512 devices in a mesh: dp: 32 (over z, x), tensor: 16 (over y, core).
Axes of the slice: x: 4, y: 8, z: 8, core: 2. Of those that a mesh axis runs over, the one named last changes fastest.
Arguments:
- x_first: bfloat16 [256, 8192], P('dp', 'tensor'), may hold values from -64 to 64
- x_second: bfloat16 [256, 8192], P('dp', 'tensor'), may hold values from -64 to 64
- cache_keys: bfloat16 [256, 128, 1024], P('dp', 'tensor'), may hold values from -512 to 512
- cache_values: bfloat16 [256, 128, 1024], P('dp', 'tensor'), may hold values from -6 to 6
- ancestors: int32 [256], replicated, may hold values from 0 to 255, as said below
- attn_gain: float32 [8192], P('tensor'), may hold values from 0.1 to 1.9
- ffn_gain: float32 [8192], P('tensor'), may hold values from 0.1 to 1.9
- w_query: bfloat16 [8192, 8192], P('tensor', 'dp'), may hold values from -0.0625 to 0.0625
- w_keyval: bfloat16 [8192, 2048], P('tensor', 'dp'), may hold values from -0.0625 to 0.0625
- w_out: bfloat16 [8192, 8192], P('dp', 'tensor'), may hold values from -0.5 to 0.5
- w_gate: bfloat16 [8192, 14336], P('tensor', 'dp'), may hold values from -0.0625 to 0.0625
- w_up: bfloat16 [8192, 14336], P('tensor', 'dp'), may hold values from -0.0625 to 0.0625
- w_down: bfloat16 [14336, 8192], P('dp', 'tensor'), may hold values from -0.046875 to 0.046875
Outputs:
- attn_update: bfloat16 [2, 256, 8192], P(None, 'dp', 'tensor')
- ffn_update: bfloat16 [2, 256, 8192], P(None, 'dp', 'tensor')
The draws below stay inside these ranges and needn't reach their ends.
Inputs may be any that keep to these rules, and one draw needn't show every extreme that they name: Particle p continues the cache of particle ancestors[p]. Among the 8 particles of one index of dp, at most 2 have ancestors in any one aligned block of 8 particles, and for every index of dp some block is named exactly 2 times.
All inputs are finite; a program needn't handle non-finite values.
Results may differ from the reference program's by a relative error of at most 0.04.
Values may be sent and summed in bfloat16 or wider, within the bound.
A program may use at most 64 MiB of HBM per device.

```python
import math
import jax
import jax.numpy as jnp
from jax import lax

D = 8192
HEADS = 64
KVH = 8
HD = 128
GROUP = 8
FF = 14336
PART_DEV = 8
PARTICLES = 256
CTX = 128
CAP = 2
N_DP = 32


def residual_rows(key):
    first, second, third = jax.random.split(key, 3)
    row_scale = jnp.exp(jax.random.uniform(first, (PARTICLES, 1), minval=math.log(0.5), maxval=math.log(5.0)))
    column = jnp.arange(D, dtype=jnp.float32) / D
    column_scale = jnp.power(3.0, column)[None, :] * jnp.exp(jax.random.uniform(second, (1, D), minval=0.0, maxval=math.log(2.0))) * 0.5
    base = jnp.clip(jax.random.normal(third, (PARTICLES, D)), -4.0, 4.0)
    return base * row_scale * column_scale


def draw_x_first(key, part):
    return residual_rows(jax.random.fold_in(key, 11)).astype(jnp.bfloat16)


def draw_x_second(key, part):
    return residual_rows(jax.random.fold_in(key, 12)).astype(jnp.bfloat16)


def draw_cache_keys(key, part):
    first = jax.random.fold_in(jax.random.fold_in(key, 21), 0)
    shape = (PARTICLES, CTX, KVH * HD)
    base = jnp.clip(jax.random.normal(first, shape), -5.0, 5.0)
    return base.astype(jnp.bfloat16)


def draw_ancestors(key, part):
    first, second, third, fourth, fifth = jax.random.split(jax.random.fold_in(key, 31), 5)
    slot_count = N_DP * CAP
    forced = jax.random.randint(first, (N_DP, 1), 0, N_DP)
    orders = jax.vmap(lambda subkey: jax.random.permutation(subkey, slot_count))(jax.random.split(second, N_DP))
    owners = jnp.arange(slot_count, dtype=jnp.int32) // CAP
    scores = orders.astype(jnp.int32) + slot_count * (owners[None, :] == forced).astype(jnp.int32)
    ranked = jnp.argsort(scores, axis=1)
    picked = owners[ranked[:, :PART_DEV - 2]]
    sources = jnp.concatenate([forced, forced, picked], axis=1)
    shuffle = jax.vmap(lambda subkey: jax.random.permutation(subkey, PART_DEV))(jax.random.split(third, N_DP))
    sources = jnp.take_along_axis(sources, shuffle, axis=1)
    local_index = jnp.minimum(jax.random.randint(fourth, (N_DP, PART_DEV), 0, PART_DEV), jax.random.randint(fifth, (N_DP, PART_DEV), 0, PART_DEV))
    return (sources * PART_DEV + local_index).reshape(PARTICLES).astype(jnp.int32)


def levels(own_key, shape, shards, smallest, top_value):
    def one(dim, shards_of):
        draws = jax.random.uniform(jax.random.fold_in(jax.random.fold_in(own_key, 6), dim), (shards_of,), jnp.float32, smallest / len(shards), top_value / len(shards))
        return jnp.repeat(jnp.exp(draws), shape[dim] // shards_of).reshape((-1,) + (1,) * (len(shape) - dim - 1))

    factor_of = one(*shards[0])
    for cut in shards[1:]:
        factor_of = factor_of * one(*cut)
    return factor_of


def noise(stream_key, extent, width, reach, shards=(), held_as=jnp.bfloat16):
    loudness = levels(stream_key, extent, shards, -0.22, 0.18) if shards else 1.0
    values = jax.random.normal(stream_key, extent, jnp.float32) * width * loudness
    return jnp.minimum(jnp.maximum(values, -reach), reach).astype(held_as)


def setup_inputs(seed: int = 0) -> dict:
    key_list = jax.random.split(jax.random.key(seed), 14)
    x_first = draw_x_first(jax.random.fold_in(key_list[13], 71), 0)
    x_second = draw_x_second(jax.random.fold_in(key_list[13], 71), 0)
    cache_keys = draw_cache_keys(jax.random.fold_in(key_list[13], 71), 0)
    cache_values = noise(key_list[3], (PARTICLES, CTX, KVH * HD), 1.0, 6.0, ((0, 32), (1, 16)))
    ancestors = draw_ancestors(jax.random.fold_in(key_list[13], 71), 0)
    attn_gain = jnp.clip(1.0 + 0.18 * jax.random.normal(key_list[5], (D,), jnp.float32), 0.1, 1.9)
    ffn_gain = jnp.clip(1.0 + 0.18 * jax.random.normal(key_list[6], (D,), jnp.float32), 0.1, 1.9)
    w_query = noise(key_list[7], (D, HEADS * HD), D ** -0.5, 0.0625, ((0, 16), (1, 32)))
    w_keyval = noise(key_list[8], (D, 2 * KVH * HD), D ** -0.5, 0.0625, ((0, 16), (1, 32)))
    w_out = noise(key_list[9], (HEADS * HD, D), (HEADS * HD // 64) ** -0.5, 0.5, ((0, 32), (1, 16)))
    w_gate = noise(key_list[10], (D, FF), D ** -0.5, 0.0625, ((0, 16), (1, 32)))
    w_up = noise(key_list[11], (D, FF), D ** -0.5, 0.0625, ((0, 16), (1, 32)))
    w_down = noise(key_list[12], (FF, D), FF ** -0.5, 0.046875, ((0, 32), (1, 16)))
    return {"x_first": x_first, "x_second": x_second, "cache_keys": cache_keys, "cache_values": cache_values, "ancestors": ancestors, "attn_gain": attn_gain, "ffn_gain": ffn_gain, "w_query": w_query, "w_keyval": w_keyval, "w_out": w_out, "w_gate": w_gate, "w_up": w_up, "w_down": w_down}


EPS = 1e-05
ROPE_BASE = 500000.0

def rounded_sum(left, right):
    return jnp.dot(left, right, preferred_element_type=jnp.float32)

def normalize(residual_in, gain):
    wide = residual_in.astype(jnp.float32)
    mean_square = lax.optimization_barrier(jnp.mean(wide * wide, axis=1, keepdims=True))
    return (wide * lax.rsqrt(mean_square + EPS) * gain[None, :]).astype(jnp.bfloat16)

def rotate(tensor, position):
    half_width = tensor.shape[-1] // 2
    freq = jnp.power(jnp.float32(ROPE_BASE), -2.0 * jnp.arange(half_width, dtype=jnp.float32) / tensor.shape[-1])
    angle = jnp.float32(position) * freq
    cosine = jnp.cos(angle)
    sine = jnp.sin(angle)
    first_half = tensor[..., :half_width]
    second_half = tensor[..., half_width:]
    return jnp.concatenate([first_half * cosine - second_half * sine, second_half * cosine + first_half * sine], axis=-1)

def project(residual_in, gain, w_query, w_keyval, position):
    normed = normalize(residual_in, gain)
    queries = rounded_sum(normed, w_query).astype(jnp.bfloat16)
    keyvals = rounded_sum(normed, w_keyval).astype(jnp.bfloat16)
    count = residual_in.shape[0]
    queries = rotate(queries.astype(jnp.float32).reshape(count, KVH, GROUP, HD), position).astype(jnp.bfloat16)
    keyvals = keyvals.reshape(count, 2, KVH, HD)
    new_keys = rotate(keyvals[:, 0].astype(jnp.float32), position).astype(jnp.bfloat16)
    return (queries, new_keys, keyvals[:, 1])

def attend(queries, keys, values):
    scale = 1.0 / math.sqrt(HD)
    scores = jnp.einsum('kgd,lkd->kgl', queries.astype(jnp.float32), keys.astype(jnp.float32), precision=lax.Precision.HIGHEST) * scale
    highest = lax.optimization_barrier(jnp.max(scores, axis=-1, keepdims=True))
    weights = jnp.exp(scores - highest)
    totals = lax.optimization_barrier(jnp.sum(weights, axis=-1))
    mixed = jnp.einsum('kgl,lkd->kgd', weights, values.astype(jnp.float32), precision=lax.Precision.HIGHEST)
    return (mixed / totals[..., None]).reshape(-1).astype(jnp.bfloat16)

def attention_all(queries, cache_keys, cache_values, sources, extra_keys, extra_values):

    def one_particle(item):
        source_row, query_one, key_more, value_more = item
        keys = jnp.concatenate([cache_keys[source_row].reshape(CTX, KVH, HD), key_more], axis=0)
        values = jnp.concatenate([cache_values[source_row].reshape(CTX, KVH, HD), value_more], axis=0)
        return attend(query_one, keys, values)
    return lax.map(one_particle, (sources, queries, extra_keys, extra_values))

def updates(residual_in, mixed, ffn_gain, w_out, w_gate, w_up, w_down):
    attn_part = rounded_sum(mixed, w_out).astype(jnp.bfloat16)
    hidden_in = (residual_in.astype(jnp.float32) + attn_part.astype(jnp.float32)).astype(jnp.bfloat16)
    normed = normalize(hidden_in, ffn_gain)
    gate = rounded_sum(normed, w_gate)
    upward = rounded_sum(normed, w_up)
    hidden = (jax.nn.silu(gate) * upward).astype(jnp.bfloat16)
    ffn_part = rounded_sum(hidden, w_down).astype(jnp.bfloat16)
    return (attn_part, ffn_part)

def reference(x_first, x_second, cache_keys, cache_values, ancestors, attn_gain, ffn_gain, w_query, w_keyval, w_out, w_gate, w_up, w_down):
    count = x_first.shape[0]
    queries_one, keys_one, values_one = project(x_first, attn_gain, w_query, w_keyval, CTX)
    queries_two, keys_two, values_two = project(x_second, attn_gain, w_query, w_keyval, CTX + 1)
    own_rows = jnp.arange(count, dtype=jnp.int32)
    mixed_one = attention_all(queries_one, cache_keys, cache_values, own_rows, keys_one[:, None], values_one[:, None])
    ancestor_rows = ancestors.astype(jnp.int32)
    extra_keys = jnp.stack([jnp.take(keys_one, ancestor_rows, axis=0), keys_two], axis=1)
    extra_values = jnp.stack([jnp.take(values_one, ancestor_rows, axis=0), values_two], axis=1)
    mixed_two = attention_all(queries_two, cache_keys, cache_values, ancestor_rows, extra_keys, extra_values)
    attn_one, ffn_one = updates(x_first, mixed_one, ffn_gain, w_out, w_gate, w_up, w_down)
    attn_two, ffn_two = updates(x_second, mixed_two, ffn_gain, w_out, w_gate, w_up, w_down)
    return (jnp.stack([attn_one, attn_two]), jnp.stack([ffn_one, ffn_two]))
```

```python
import math

import jax
import jax.numpy as jnp
from jax import lax
from jax.sharding import Mesh, PartitionSpec as P

NZ, NX, NY, NC = 8, 4, 8, 2
HD = 128
GROUP = 8
EPS = 1e-05
ROPE_BASE = 500000.0
DP = ("z", "x")
TENSOR = ("y", "c")
F32 = jnp.float32
BF16 = jnp.bfloat16
LOW = -1e30


def exchange(blocks, axes):
    return lax.all_to_all(blocks, axes, split_axis=0, concat_axis=0, tiled=True)


def spread(block, axes, count):
    return exchange(jnp.broadcast_to(block[None], (count, *block.shape)), axes)


def dot(a, b):
    return jnp.dot(a, b, preferred_element_type=F32)


def split_hi_lo(value):
    hi = value.astype(BF16)
    return hi, (value - hi.astype(F32)).astype(BF16)


def tables(ancestors, block, half):
    anc = ancestors.reshape(NZ * NX, 8)
    earlier = jnp.tril(jnp.ones((8, 8), jnp.int32), -1)
    mine = lax.dynamic_index_in_dim(anc, block, 0, keepdims=False)
    mine_block, mine_half = mine // 8, (mine // 4) % 2
    quad = mine // 4
    rank = jnp.sum((quad[:, None] == quad[None, :]) * earlier, axis=1)
    i = jnp.arange(NZ * NX)[:, None, None, None]
    head = jnp.arange(8)[None, :, None, None]
    slot = jnp.arange(2)[None, None, :, None]
    col = jnp.arange(128)[None, None, None, :]
    particle = (col // 8) % 2 * 4 + col % 4
    col_block, col_half, col_rank = (
        jnp.broadcast_to(v.reshape(1, 2, 1, 4), (8, 2, 2, 4)).reshape(1, 1, 1, 128)
        for v in (mine_block, mine_half, rank)
    )
    hit = (
        (col // 16 == head)
        & ((col // 4) % 2 == 1)
        & (col_block == i)
        & (col_half == half)
        & (col_rank == slot)
        & (particle >= 0)
    )
    select = hit.astype(BF16).reshape(512, 128)
    wanted = anc // 4 == block * 2 + half
    order = jnp.sum(wanted[:, None, :] * earlier[None], axis=2)
    which = jnp.stack(
        [jnp.sum(jnp.where(wanted & (order == s), anc % 4, 0), axis=1) for s in range(2)], axis=1
    )
    which = jnp.broadcast_to(which[:, None, :], (NZ * NX, 8, 2)).reshape(512, 1)
    own = jnp.broadcast_to(jnp.arange(128)[:, None] % 4, (128, 1))
    return select, jnp.concatenate([which, own], axis=0).astype(jnp.int32)


def angles(position):
    freq = jnp.power(F32(ROPE_BASE), -2.0 * jnp.arange(HD // 2, dtype=F32) / HD)
    angle = F32(position) * freq
    return jnp.cos(angle), jnp.sin(angle)


def rotate(rows, context):
    tables_ = [angles(context), angles(context + 1)]
    cos = jnp.stack([jnp.concatenate([c, c]) for c, _ in tables_])
    sin = jnp.stack([jnp.concatenate([-s, s]) for _, s in tables_])
    step = (jnp.arange(rows.shape[0]) // 4) % 2
    cos = jnp.where(step[:, None] == 0, cos[0], cos[1])
    sin = jnp.where(step[:, None] == 0, sin[0], sin[1])
    turned = jnp.concatenate([rows[:, 64:], rows[:, :64]], axis=1)
    return rows * cos + turned * sin


def attend(queries, keys, values, which, own_key, own_value, half):
    scale = 1.0 / math.sqrt(HD)
    scores = lax.dot_general(
        queries, keys, (((1,), (1,)), ((), ())), preferred_element_type=F32
    ) * scale
    k = jnp.arange(640)[None, :]
    new = k - 512
    key_particle = jnp.where(k < 512, (k // 8) % 4, k % 4)
    key_ok = (k < 512) | ((new < 16) & ((new // 4) % 2 == 0) & (new // 8 == half))
    scores = jnp.where((key_particle == which) & key_ok, scores, LOW)
    own = jnp.sum(queries[:512].astype(F32) * own_key, axis=1, keepdims=True) * scale
    own = jnp.concatenate([own, jnp.full((128, 1), LOW, F32)], axis=0)
    highest = jnp.maximum(jnp.max(scores, axis=1, keepdims=True), own)
    weights = jnp.exp(scores - highest)
    own = jnp.exp(own - highest)
    totals = jnp.sum(weights, axis=1, keepdims=True) + own
    mixed = dot(weights.astype(BF16), values)
    extra = jnp.concatenate([own[:512] * own_value, jnp.zeros((128, HD), F32)], axis=0)
    return ((mixed + extra) / totals).astype(BF16)


def sum_blocks(blocks):
    return jnp.sum(blocks.astype(F32), axis=0)


def local(
    x_first, x_second, cache_keys, cache_values, ancestors, attn_gain, ffn_gain,
    w_query, w_keyval, w_out, w_gate, w_up, w_down,
):
    z, x, y, c = (lax.axis_index(a) for a in ("z", "x", "y", "c"))
    context = cache_keys.shape[1] * NY * NC
    width = x_first.shape[1] * NY * NC
    dp, ff = NZ * NX, w_gate.shape[1]
    select, which = tables(ancestors, y * NX + x, c)

    cache = jnp.stack([cache_keys, cache_values]).reshape(2, 8, 8, 8, HD)
    cache = exchange(cache.transpose(3, 0, 1, 2, 4), ("z",))
    cache = cache.reshape(8, 2, 2, 4, 8, HD).transpose(0, 2, 1, 3, 4, 5).reshape(16, 2, 32, HD)
    cache = exchange(cache, TENSOR).transpose(1, 0, 2, 3).reshape(2, 512, HD)

    moves = [(s, (s % 16) // 2 * NX + s // 16 * 2 + s % 2) for s in range(dp)]
    w_keyval = lax.ppermute(w_keyval, DP, moves)

    rows = jnp.stack([x_first.reshape(2, 4, -1), x_second.reshape(2, 4, -1)], axis=1).reshape(16, -1)
    wide = spread(rows, DP, dp).reshape(512, -1).astype(F32)
    squares = jnp.concatenate(split_hi_lo(jnp.sum(wide * wide, axis=1, keepdims=True)), axis=1)
    scaled = (wide * attn_gain[None, :]).astype(BF16)
    part = dot(scaled, jnp.concatenate([w_query, w_keyval], axis=1)).astype(BF16)
    part = jnp.concatenate([part, jnp.pad(squares, ((0, 0), (0, 62)))], axis=1)
    part = part.reshape(NZ, NX, 2, 8, 384).transpose(0, 2, 1, 3, 4).reshape(16, 32, 384)
    total = sum_blocks(exchange(part, TENSOR))
    factor = lax.rsqrt((total[:, 320:321] + total[:, 321:322]) / width + EPS)
    heads = (total[:, :320] * factor).astype(BF16).reshape(NX, 1, 8, 320)
    heads = exchange(jnp.broadcast_to(heads, (NX, NC, 8, 320)).reshape(8, 8, 320), ("x", "c"))
    heads = heads.reshape(NX, 16, 320).astype(F32)

    queries = heads[:, :, :256].reshape(NX, 16, 2, HD).transpose(0, 2, 1, 3).reshape(128, HD)
    queries = rotate(queries, context).astype(BF16)
    new_keys = rotate(jnp.concatenate([heads[0, :, 256:], heads[1, :, 256:]], axis=1), context)
    new_keys = new_keys.astype(BF16)
    new_values = jnp.concatenate([heads[2, :, 256:], heads[3, :, 256:]], axis=1).astype(BF16)

    pairs = jnp.concatenate([new_keys, new_values, jnp.zeros((96, HD), BF16)], axis=0)
    send = jnp.concatenate([dot(select, queries), dot(select, pairs_for(pairs))], axis=1)
    got = exchange(send.astype(BF16).reshape(dp, 16, 256), ("y", "x")).reshape(512, 256)
    row = jnp.arange(512)[:, None]
    col = jnp.arange(512)[None, :]
    same = (row // 16 == col // 16) & (row % 2 == col % 2)
    own_key = dot((same & (col // 2 % 8 == 0)).astype(BF16), got[:, HD:])
    own_value = dot((same & (col // 2 % 8 == 1)).astype(BF16), got[:, HD:])
    pad = jnp.zeros((112, HD), BF16)
    mixed = attend(
        jnp.concatenate([got[:, :HD], queries], axis=0),
        jnp.concatenate([cache[0], new_keys, pad], axis=0),
        jnp.concatenate([cache[1], new_values, pad], axis=0),
        which, own_key, own_value, c,
    )
    back = exchange(mixed[:512].reshape(dp, 16, HD), ("y", "x")).reshape(512, HD)
    second = lax.dot_general(select, back, (((0,), (0,)), ((), ())), preferred_element_type=F32)
    r = jnp.arange(128)[:, None]
    first = jnp.where(((r // 4) % 2 == 0) & ((r // 8) % 2 == c), mixed[512:].astype(F32), 0.0)
    mixed = (first + second).astype(BF16).reshape(NX, 2, 16, HD).transpose(0, 2, 1, 3)
    mixed = mixed.reshape(NX, 1, 16, 256)
    mixed = exchange(jnp.broadcast_to(mixed, (NX, NC, 16, 256)).reshape(8, 16, 256), ("x", "c"))
    mixed = jnp.sum(mixed.reshape(NX, NC, 16, 256), axis=1).reshape(64, 256)
    mixed = spread(mixed, ("y",), NY).reshape(512, 256)

    part = dot(mixed, w_out).astype(BF16).reshape(dp, 16, -1)
    attn = sum_blocks(exchange(part, DP)).astype(BF16)
    residual = (rows.astype(F32) + attn.astype(F32)).astype(BF16)

    wide = spread(residual, DP, dp).reshape(512, -1).astype(F32)
    squares = jnp.concatenate(split_hi_lo(jnp.sum(wide * wide, axis=1, keepdims=True)), axis=1)
    scaled = (wide * ffn_gain[None, :]).astype(BF16)
    gate = jnp.concatenate(
        [dot(scaled, w_gate).astype(BF16), jnp.pad(squares, ((0, 0), (0, 62)))], axis=1
    )
    up = jnp.pad(dot(scaled, w_up).astype(BF16), ((0, 0), (0, 64)))
    part = jnp.concatenate([gate, up], axis=1).reshape(16, 32, 2 * (ff + 64))
    total = sum_blocks(exchange(part, TENSOR))
    factor = lax.rsqrt((total[:, ff : ff + 1] + total[:, ff + 1 : ff + 2]) / width + EPS)
    gate, up = total[:, :ff] * factor, total[:, ff + 64 : 2 * ff + 64] * factor
    hidden = (gate / (1.0 + jnp.exp(-gate)) * up).astype(BF16)
    hidden = spread(hidden, TENSOR, NY * NC).reshape(512, ff)
    part = dot(hidden, w_down).astype(BF16).reshape(dp, 16, -1)
    ffn = sum_blocks(exchange(part, DP)).astype(BF16)

    def by_step(block):
        return block.reshape(2, 2, 4, -1).transpose(1, 0, 2, 3).reshape(2, 8, -1)

    return by_step(attn), by_step(ffn)


def pairs_for(pairs):
    return jnp.concatenate([pairs[:32], jnp.zeros((96, HD), BF16)], axis=0)


def solution(mesh):
    fine = Mesh(mesh.devices.reshape(NZ, NX, NY, NC), ("z", "x", "y", "c"))
    rows, cols = P(TENSOR, DP), P(DP, TENSOR)
    return jax.shard_map(
        local,
        mesh=fine,
        in_specs=(
            cols, cols, P(DP, TENSOR, None), P(DP, TENSOR, None), P(), P(TENSOR), P(TENSOR),
            rows, rows, cols, rows, rows, cols,
        ),
        out_specs=(P(None, DP, TENSOR), P(None, DP, TENSOR)),
        check_vma=False,
    )
```

```python
import functools
import math

import jax
import jax.numpy as jnp
import numpy as np
from jax import lax
from jax.experimental import pallas as pl
from jax.experimental.pallas import tpu as pltpu
from jax.sharding import Mesh, PartitionSpec as P

NZ, NX, NY, NC = 8, 4, 8, 2
HD = 128
EPS = 1e-05
ROPE_BASE = 500000.0
DP = ("z", "x")
TENSOR = ("y", "c")
F32 = jnp.float32
BF16 = jnp.bfloat16
LOW = -1e30
MESH = pl.DeviceIdType.MESH


def dot(a, b):
    return jnp.dot(a, b, preferred_element_type=F32)


def tables(ancestors, block, half):
    anc = ancestors.reshape(NZ * NX, 8)
    earlier = jnp.tril(jnp.ones((8, 8), jnp.int32), -1)
    mine = lax.dynamic_index_in_dim(anc, block, 0, keepdims=False)
    mine_block, mine_half = mine // 8, (mine // 4) % 2
    quad = mine // 4
    rank = jnp.sum((quad[:, None] == quad[None, :]) * earlier, axis=1)
    place = (mine_block % NX) * NZ + mine_block // NX
    row = jnp.arange(512)[:, None]
    col = jnp.arange(128)[None, :]
    col_place, col_half, col_rank = (
        jnp.broadcast_to(v.reshape(1, 2, 1, 4), (8, 2, 2, 4)).reshape(1, 128)
        for v in (place, mine_half, rank)
    )
    hit = (
        (col // 16 == row // 2 % 8)
        & ((col // 4) % 2 == 1)
        & (col_place == row // 16)
        & (col_half == half)
        & (col_rank == row % 2)
    )
    select = hit.astype(BF16)
    wanted = anc // 4 == block * 2 + half
    order = jnp.sum(wanted[:, None, :] * earlier[None], axis=2)
    which = jnp.stack(
        [jnp.sum(jnp.where(wanted & (order == s), anc % 4, 0), axis=1) for s in range(2)], axis=1
    )
    which = which.reshape(NZ, NX, 1, 2).transpose(1, 0, 2, 3)
    which = jnp.broadcast_to(which, (NX, NZ, 8, 2)).reshape(512, 1)
    own = jnp.arange(128)[:, None] % 4
    return select, select.T, jnp.concatenate([which, own], axis=0).astype(jnp.int32)


def angles(context):
    freq = np.power(np.float32(ROPE_BASE), -2.0 * np.arange(HD // 2, dtype=np.float32) / HD)
    freq = freq.astype(np.float32)
    step = (np.arange(16) // 4) % 2
    angle = (np.float32(context) + step.astype(np.float32))[:, None] * freq[None, :]
    cos, sin = np.cos(angle), np.sin(angle)
    both = np.stack([np.concatenate([cos, cos], 1), np.concatenate([-sin, sin], 1)])
    return jnp.asarray(both.astype(np.float32))


def iota(shape, dim):
    return lax.broadcasted_iota(jnp.int32, shape, dim)


def kernel(
    xrow, select, select_t, which, attn_gain, ffn_gain, rope, ck, cv, wq, wkv, wo, wg, wu, wd,
    attn_out, ffn_out,
    wq_v, wkv_r, wkv_p, wo_v, wg_r, wu_r, wgu_v, wd_v,
    ga, gg, part, bcs, bcr, bys, byr, cs, cr, cache1, cache2,
    ds_, dr, rs, rr, es, er, mb, fxs, fxr, fzs, fzr, ixs, ixr, izs, izr,
    hown, hcs, hcr, hys, hyr, hid,
    lsem, kvsem, gaz, gax, ggz, ggx, bc, by, csem, c1, c2, dsem, rsem, esem, e2sem,
    fx, fz, ix, iz, hc, hy, h2y, h2c,
):
    z, x, y, c = (lax.axis_index(a) for a in ("z", "x", "y", "c"))
    width = xrow.shape[1] * NY * NC
    ff = wg.shape[1]
    finals = []

    def loop(low, high, body):
        def step(k, carry):
            body(k)
            return carry

        lax.fori_loop(low, high, step, 0)

    def remote(src, dst, sems, n, **where):
        return pltpu.make_async_remote_copy(
            src_ref=src, dst_ref=dst, send_sem=sems.at[0, n], recv_sem=sems.at[1, n],
            device_id=where, device_id_type=MESH,
        )

    def arrived(ref, sems, n):
        pltpu.make_async_copy(ref, ref, sems.at[1, n]).wait()

    def sent(ref, sems, n):
        pltpu.make_async_copy(ref, ref, sems.at[0, n]).wait()

    zk = lambda k: lax.rem(z + k, NZ)
    zb = lambda k: lax.rem(z + NZ - k, NZ)
    xk = lambda j: lax.rem(x + j, NX)
    xb = lambda j: lax.rem(x + NX - j, NX)
    yk = lambda k: lax.rem(y + k, NY)
    yb = lambda k: lax.rem(y + NY - k, NY)

    loads = [
        pltpu.make_async_copy(wq, wq_v, lsem.at[0]),
        pltpu.make_async_copy(wo, wo_v, lsem.at[1]),
        pltpu.make_async_copy(wg, wg_r, lsem.at[2]),
        pltpu.make_async_copy(wu, wu_r, lsem.at[3]),
        pltpu.make_async_copy(wd, wd_v.at[pl.ds(0, ff)], lsem.at[4]),
        pltpu.make_async_copy(ck.at[:, pl.ds(pl.multiple_of(z * HD, HD), HD)], cache1.at[z, 0], lsem.at[5]),
        pltpu.make_async_copy(cv.at[:, pl.ds(pl.multiple_of(z * HD, HD), HD)], cache1.at[z, 1], lsem.at[6]),
    ]
    for load in loads:
        load.start()
    ga[x, z] = xrow[...]

    me = z * NX + x
    to_z, to_x = (me % 16) // 2, me // 16 * 2 + me % 2
    from_dp = x // 2 * 16 + 2 * z + x % 2
    from_z, from_x = from_dp // NX, from_dp % NX
    stays = from_dp == me
    barrier = pltpu.get_barrier_semaphore()

    def greet(**where):
        pl.semaphore_signal(barrier, inc=1, device_id=where, device_id_type=MESH)

    loop(1, 8, lambda k: greet(z=zk(k)))
    loop(1, 32, lambda n: greet(x=xk(n // 8), y=yk(n % 8)))
    loop(0, 4, lambda j: greet(x=xk(j), c=1 - c))
    loop(1, 8, lambda k: greet(y=yk(k), c=1 - c))

    @pl.when(jnp.logical_not(stays))
    def _():
        greet(z=to_z, x=to_x)
        greet(z=from_z, x=from_x)

    pl.semaphore_wait(barrier, jnp.where(stays, 49, 51))

    def gather_begin(buf, zs, xs):
        loop(1, 8, lambda k: remote(buf.at[x, z], buf.at[x, z], zs, k, z=zk(k)).start())
        loop(1, 4, lambda j: remote(buf.at[x, z], buf.at[x, z], xs, j, x=xk(j)).start())

    def gather_end(buf, zs, xs):
        def pass_on(k):
            block = buf.at[x, zb(k)]
            arrived(block, zs, k)
            loop(1, 4, lambda j: remote(block, block, xs, k * 4 + j, x=xk(j)).start())

        loop(1, 8, pass_on)
        loop(0, 8, lambda k: loop(1, 4, lambda j: arrived(buf.at[xb(j), zb(k)], xs, k * 4 + j)))

        def close():
            loop(1, 8, lambda k: sent(buf.at[x, z], zs, k))
            loop(0, 8, lambda k: loop(1, 4, lambda j: sent(buf.at[x, z], xs, k * 4 + j)))

        finals.append(close)

    def scatter_dp(xsend, xrecv, zsend, zrecv, xs, zs):
        def out(k):
            loop(1, 4, lambda j: remote(
                xsend.at[xk(j), zk(k + 1)], xrecv.at[x, zk(k + 1)], xs, lax.rem(k + 1, 8) * 4 + j, x=xk(j)
            ).start())

        loop(0, 8, out)

        def total(k):
            block = xsend[x, zk(k)].astype(F32)
            for j in range(1, 4):
                arrived(xrecv.at[xb(j), zk(k)], xs, k * 4 + j)
                block = block + xrecv[xb(j), zk(k)].astype(F32)
            return block

        def pass_on(k):
            zsend[zk(k)] = total(k).astype(BF16)
            remote(zsend.at[zk(k)], zrecv.at[z], zs, k, z=zk(k)).start()

        loop(1, 8, pass_on)
        acc = total(0)
        for k in range(1, 8):
            arrived(zrecv.at[zb(k)], zs, k)
            acc = acc + zrecv[zb(k)].astype(F32)

        def close():
            loop(0, 8, lambda k: loop(1, 4, lambda j: sent(xsend.at[0, 0], xs, k * 4 + j)))
            loop(1, 8, lambda k: sent(zsend.at[0], zs, k))

        finals.append(close)
        return acc

    def scatter_tensor(own, csend, crecv, ysend, yrecv, cs_, ys_, between):
        def pass_on(k):
            n = yk(k)
            arrived(crecv.at[n], cs_, k)
            ysend[n] = (own(n) + crecv[n].astype(F32)).astype(BF16)
            remote(ysend.at[n], yrecv.at[y], ys_, k, y=n).start()

        loop(1, 8, pass_on)
        arrived(crecv.at[y], cs_, 0)
        between()
        acc = own(y) + crecv[y].astype(F32)
        for k in range(1, 8):
            arrived(yrecv.at[yb(k)], ys_, k)
            acc = acc + yrecv[yb(k)].astype(F32)

        def close():
            loop(0, 8, lambda k: sent(csend.at[0], cs_, k))
            loop(1, 8, lambda k: sent(ysend.at[0], ys_, k))

        finals.append(close)
        return acc

    gather_begin(ga, gaz, gax)

    @pl.when(stays)
    def _():
        pltpu.make_async_copy(wkv, wkv_r, kvsem.at[1, 0]).start()

    @pl.when(jnp.logical_not(stays))
    def _():
        remote(wkv, wkv_r, kvsem, 0, z=to_z, x=to_x).start()

    def cache_out(k):
        cols = pl.ds(pl.multiple_of(zk(k) * HD, HD), HD)
        remote(ck.at[:, cols], cache1.at[z, 0], c1, k, z=zk(k)).start()
        remote(cv.at[:, cols], cache1.at[z, 1], c1, 8 + k, z=zk(k)).start()

    loop(1, 8, cache_out)

    wd_v[pl.ds(ff, 512 - ff), :] = jnp.zeros((512 - ff, 512), BF16)
    wgu_v[...] = jnp.zeros_like(wgu_v)
    wkv_p[...] = jnp.zeros_like(wkv_p)
    loads[2].wait()
    loads[3].wait()
    wgu_v[:, 0:ff] = wg_r[...]
    wgu_v[:, 512 : 512 + ff] = wu_r[...]
    gather_end(ga, gaz, gax)
    loads[0].wait()
    arrived(wkv_r, kvsem, 0)
    wkv_p[:, 0:64] = wkv_r[...]

    lane = iota((128, 128), 1)

    def squares_of(wide):
        square = jnp.sum(wide * wide, axis=1, keepdims=True)
        hi = square.astype(BF16).astype(F32)
        return jnp.where(lane == 64, hi, 0.0) + jnp.where(lane == 65, square - hi, 0.0)

    def project(n):
        wide = ga[n].reshape(128, 512).astype(F32)
        scaled = (wide * attn_gain[...]).astype(BF16)
        part[n, :, :, :, 0:256] = dot(scaled, wq_v[...]).reshape(8, 2, 8, 256)
        part[n, :, :, :, 256:384] = (dot(scaled, wkv_p[...]) + squares_of(wide)).reshape(8, 2, 8, 128)

    loop(0, 4, project)

    def to_core(k):
        n = yk(k + 1)
        bcs[n] = part[:, n, 1 - c].reshape(32, 384).astype(BF16)
        remote(bcs.at[n], bcr.at[n], bc, lax.rem(k + 1, 8), c=1 - c).start()

    loop(0, 8, to_core)

    def cache_pass():
        loads[5].wait()
        loads[6].wait()

        def came(k):
            arrived(cache1.at[zb(k), 0], c1, k)
            arrived(cache1.at[zb(k), 1], c1, 8 + k)

        loop(1, 8, came)
        other = 1 - c
        keep = pltpu.make_async_copy(
            cache1.at[y, :, pl.ds(pl.multiple_of(c * 32, 32), 32), :], cache2.at[y * 2 + c], lsem.at[7]
        )
        keep.start()

        def pass_same(k):
            remote(
                cache1.at[yk(k), :, pl.ds(pl.multiple_of(c * 32, 32), 32), :], cache2.at[y * 2 + c],
                c2, k, y=yk(k),
            ).start()

        loop(1, 8, pass_same)

        def pass_other(k):
            remote(
                cache1.at[yk(k), :, pl.ds(pl.multiple_of(other * 32, 32), 32), :], cache2.at[y * 2 + c],
                c2, 8 + k, y=yk(k), c=other,
            ).start()

        loop(0, 8, pass_other)
        keep.wait()

        def close():
            loop(1, 8, lambda k: sent(cache1.at[0, 0], c1, k))
            loop(1, 8, lambda k: sent(cache1.at[0, 0], c1, 8 + k))
            loop(1, 16, lambda k: sent(cache2.at[0], c2, k))

            @pl.when(jnp.logical_not(stays))
            def _():
                sent(wkv_r, kvsem, 0)

        finals.append(close)

    acc = scatter_tensor(
        lambda n: part[:, n, c].reshape(32, 384), bcs, bcr, bys, byr, bc, by, cache_pass
    )
    factor = lax.rsqrt((acc[:, 320:321] + acc[:, 321:322]) / width + EPS)
    cs[...] = (acc * factor).astype(BF16).astype(F32).reshape(4, 8, 384)

    def share(src, dst, sems):
        def one(n):
            j, e = n // 2, n % 2
            to_c = lax.rem(c + e, 2)
            remote(src.at[xk(j)], dst.at[x, c], sems, n, x=xk(j), c=to_c).start()

        dst[x, c] = src[x]
        loop(1, 8, one)
        loop(1, 8, lambda n: arrived(dst.at[xb(n // 2), lax.rem(c + n % 2, 2)], sems, n))
        finals.append(lambda: loop(1, 8, lambda n: sent(src.at[0], sems, n)))

    share(cs, cr, csem)

    def rotated(rows):
        count = rows.shape[0] // 16
        cos = jnp.concatenate([rope[0]] * count, axis=0)
        sin = jnp.concatenate([rope[1]] * count, axis=0)
        return (rows * cos + pltpu.roll(rows, 64, 1) * sin).astype(BF16)

    heads = [cr[n].reshape(16, 384) for n in range(4)]
    queries = rotated(
        jnp.concatenate([h[:, a : a + HD] for h in heads for a in (0, HD)], axis=0)
    )
    low = iota((16, HD), 1) < 64
    join = lambda a, b: jnp.where(low, a[:, 256:384], pltpu.roll(b[:, 256:384], 64, 1))
    new_keys = rotated(join(heads[0], heads[1]))
    new_values = join(heads[2], heads[3]).astype(BF16)

    spot = x * 8 + y
    pairs = jnp.concatenate([new_keys, new_values, jnp.zeros((96, HD), BF16)], axis=0)
    ds_[:, :, 0:HD] = dot(select[...], queries).astype(BF16).reshape(32, 16, HD)
    ds_[:, :, HD : 2 * HD] = dot(select[...], pairs).astype(BF16).reshape(32, 16, HD)
    dr[spot] = ds_[spot]

    def trade(src, dst, sems):
        def one(n):
            px, py = xk(n // 8), yk(n % 8)
            remote(src.at[px * 8 + py], dst.at[spot], sems, n, x=px, y=py).start()

        loop(1, 32, one)
        finals.append(lambda: loop(1, 32, lambda n: sent(src.at[0], sems, n)))

    def traded(dst, sems):
        loop(1, 32, lambda n: arrived(dst.at[xb(n // 8) * 8 + yb(n % 8)], sems, n))

    trade(ds_, dr, dsem)
    loop(1, 16, lambda k: arrived(cache2.at[yb(lax.rem(k, 8)) * 2 + lax.rem(c + k // 8, 2)], c2, k))
    traded(dr, dsem)

    row = iota((512, 512), 0)
    col = iota((512, 512), 1)
    same = (row // 16 == col // 16) & (row % 2 == col % 2)
    kind = col // 2 % 8
    tail = dr[:, :, HD : 2 * HD].reshape(512, HD)
    own_key = dot(jnp.where(same & (kind == 0), 1.0, 0.0).astype(BF16), tail)
    own_value = dot(jnp.where(same & (kind == 1), 1.0, 0.0).astype(BF16), tail)
    asked = jnp.concatenate([dr[:, :, 0:HD].reshape(512, HD), queries], axis=0)
    pad = jnp.zeros((112, HD), BF16)
    keys = jnp.concatenate([cache2[:, 0].reshape(512, HD), new_keys, pad], axis=0)
    values = jnp.concatenate([cache2[:, 1].reshape(512, HD), new_values, pad], axis=0)
    scale = 1.0 / math.sqrt(HD)
    scores = lax.dot_general(asked, keys, (((1,), (1,)), ((), ())), preferred_element_type=F32)
    k = iota((1, 640), 1)
    new = k - 512
    key_particle = jnp.where(k < 512, (k // 8) % 4, k % 4)
    key_ok = (k < 512) | ((new < 16) & ((new // 4) % 2 == 0) & (new // 8 == c))
    key_particle = jnp.where(key_ok, key_particle, -1)
    scores = jnp.where(key_particle == which[...], scores * scale, LOW)
    own = jnp.sum(asked[0:512].astype(F32) * own_key, axis=1, keepdims=True) * scale
    own = jnp.concatenate([own, jnp.full((128, 1), LOW, F32)], axis=0)
    highest = jnp.maximum(jnp.max(scores, axis=1, keepdims=True), own)
    weights = jnp.exp(scores - highest)
    own = jnp.exp(own - highest)
    totals = jnp.sum(weights, axis=1, keepdims=True) + own
    mixed = dot(weights.astype(BF16), values)
    extra = jnp.concatenate([own[0:512] * own_value, jnp.zeros((128, HD), F32)], axis=0)
    mixed = (mixed + extra) / totals

    rs[...] = mixed[0:512].astype(BF16).reshape(32, 16, HD)
    rr[spot] = rs[spot]
    trade(rs, rr, rsem)
    r = iota((128, 1), 0)
    first = jnp.where(((r // 4) % 2 == 0) & ((r // 8) % 2 == c), mixed[512:640], 0.0)
    traded(rr, rsem)
    both = (first + dot(select_t[...], rr[...].reshape(512, HD))).astype(BF16)
    for n in range(4):
        es[n, :, 0:HD] = both[n * 32 : n * 32 + 16]
        es[n, :, HD : 2 * HD] = both[n * 32 + 16 : n * 32 + 32]
    share(es, er, esem)
    mb[y] = (er[:, 0].astype(F32) + er[:, 1].astype(F32)).astype(BF16).reshape(64, 256)
    loop(1, 8, lambda k: remote(mb.at[y], mb.at[y], e2sem, k, y=yk(k)).start())
    finals.append(lambda: loop(1, 8, lambda k: sent(mb.at[0], e2sem, k)))
    loads[1].wait()
    loop(1, 8, lambda k: arrived(mb.at[yb(k)], e2sem, k))

    for n in range(4):
        rows = mb[:, n * 16 : n * 16 + 16, :].reshape(128, 256)
        fxs[n] = dot(rows, wo_v[...]).astype(BF16).reshape(8, 16, 512)
    attn = scatter_dp(fxs, fxr, fzs, fzr, fx, fz).astype(BF16)
    attn_out[...] = attn
    gg[x, z] = (xrow[...].astype(F32) + attn.astype(F32)).astype(BF16)

    gather_begin(gg, ggz, ggx)
    gather_end(gg, ggz, ggx)

    def gate_up(n):
        wide = gg[n].reshape(128, 512).astype(F32)
        scaled = (wide * ffn_gain[...]).astype(BF16)
        return dot(scaled, wgu_v[...]), squares_of(wide)

    for n in range(2):
        value, square = gate_up(2 * (1 - c) + n)
        at = slice(n * 16, n * 16 + 16)
        hcs[:, at, :] = value.astype(BF16).reshape(8, 16, 1024)
        hcs[:, at, 384:512] = (value[:, 384:512] + square).astype(BF16).reshape(8, 16, 128)

    def to_core_again(k):
        n = yk(k + 1)
        remote(hcs.at[n], hcr.at[n], hc, lax.rem(k + 1, 8), c=1 - c).start()

    loop(0, 8, to_core_again)
    for n in range(2):
        value, square = gate_up(2 * c + n)
        at = slice(n * 16, n * 16 + 16)
        hown[:, at, :] = value.reshape(8, 16, 1024)
        hown[:, at, 384:512] = (value[:, 384:512] + square).reshape(8, 16, 128)
    acc = scatter_tensor(lambda n: hown[n], hcs, hcr, hys, hyr, hc, hy, lambda: None)
    factor = lax.rsqrt((acc[:, ff : ff + 1] + acc[:, ff + 1 : ff + 2]) / width + EPS)
    gate, up = acc[:, 0:512] * factor, acc[:, 512:1024] * factor
    hidden = gate / (1.0 + jnp.exp(-gate)) * up
    hid[c, y] = jnp.where(iota((32, 512), 1) < ff, hidden, 0.0).astype(BF16)

    loop(1, 8, lambda k: remote(hid.at[c, y], hid.at[c, y], h2y, k, y=yk(k)).start())
    remote(hid.at[c, y], hid.at[c, y], h2c, 0, c=1 - c).start()

    def pass_hidden(k):
        block = hid.at[c, yb(k)]
        arrived(block, h2y, k)
        remote(block, block, h2c, k, c=1 - c).start()

    loop(1, 8, pass_hidden)
    loads[4].wait()
    loop(0, 8, lambda k: arrived(hid.at[1 - c, yb(k)], h2c, k))

    for n in range(4):
        rows = hid[n // 2, :, (n % 2) * 16 : (n % 2) * 16 + 16, :].reshape(128, 512)
        ixs[n] = dot(rows, wd_v[...]).astype(BF16).reshape(8, 16, 512)
    ffn_out[...] = scatter_dp(ixs, ixr, izs, izr, ix, iz).astype(BF16)

    loop(1, 8, lambda k: sent(hid.at[0, 0], h2y, k))
    loop(0, 8, lambda k: sent(hid.at[0, 0], h2c, k))
    for close in finals:
        close()


def local(
    x_first, x_second, cache_keys, cache_values, ancestors, attn_gain, ffn_gain,
    w_query, w_keyval, w_out, w_gate, w_up, w_down,
):
    z, x, y, c = (lax.axis_index(a) for a in ("z", "x", "y", "c"))
    context = cache_keys.shape[1] * NY * NC
    select, select_t, which = tables(ancestors, y * NX + x, c)
    rows = jnp.stack([x_first.reshape(2, 4, -1), x_second.reshape(2, 4, -1)], axis=1).reshape(16, -1)
    v = lambda *shape: pltpu.VMEM(shape, BF16)
    f = lambda *shape: pltpu.VMEM(shape, F32)
    sem = lambda n: pltpu.SemaphoreType.DMA((2, n))
    near, far = pl.BlockSpec(memory_space=pltpu.VMEM), pl.BlockSpec(memory_space=pl.ANY)
    big = [v(4, 8, 16, 512), v(4, 8, 16, 512), v(8, 16, 512), v(8, 16, 512)]
    attn, ffn = pl.pallas_call(
        kernel,
        out_shape=[jax.ShapeDtypeStruct((16, 512), BF16)] * 2,
        in_specs=[near] * 7 + [far] * 8,
        out_specs=[near, near],
        scratch_shapes=[
            v(512, 256), v(512, 64), v(512, 128), v(256, 512), v(512, 448), v(512, 448), v(512, 1024),
            v(512, 512),
            v(4, 8, 16, 512), v(4, 8, 16, 512), f(4, 8, 2, 8, 384),
            *[v(8, 32, 384)] * 4,
            f(4, 8, 384), f(4, 2, 8, 384), v(8, 2, 64, HD), v(16, 2, 32, HD),
            v(32, 16, 256), v(32, 16, 256), v(32, 16, HD), v(32, 16, HD),
            v(4, 16, 256), v(4, 2, 16, 256), v(8, 64, 256),
            *big, *big,
            f(8, 32, 1024), *[v(8, 32, 1024)] * 4, v(2, 8, 32, 512),
            pltpu.SemaphoreType.DMA((8,)), sem(1), sem(8), sem(32), sem(8), sem(32), sem(8), sem(8),
            sem(8), sem(16), sem(16), sem(32), sem(32), sem(8), sem(8),
            sem(32), sem(8), sem(32), sem(8), sem(8), sem(8), sem(8), sem(8),
        ],
        compiler_params=pltpu.CompilerParams(
            collective_id=0, has_side_effects=True, vmem_limit_bytes=48 * 2**20
        ),
        cost_estimate=pl.CostEstimate(flops=2**30, bytes_accessed=2**22, transcendentals=2**19),
    )(
        rows, select, select_t, which, attn_gain[None], ffn_gain[None], angles(context),
        cache_keys.reshape(64, -1), cache_values.reshape(64, -1),
        w_query, w_keyval, w_out, w_gate, w_up, w_down,
    )

    def by_step(block):
        return block.reshape(2, 2, 4, -1).transpose(1, 0, 2, 3).reshape(2, 8, -1)

    return by_step(attn), by_step(ffn)


def solution(mesh):
    fine = Mesh(mesh.devices.reshape(NZ, NX, NY, NC), ("z", "x", "y", "c"))
    rows, cols = P(TENSOR, DP), P(DP, TENSOR)
    return jax.shard_map(
        local,
        mesh=fine,
        in_specs=(
            cols, cols, P(DP, TENSOR, None), P(DP, TENSOR, None), P(), P(TENSOR), P(TENSOR),
            rows, rows, cols, rows, rows, cols,
        ),
        out_specs=(P(None, DP, TENSOR), P(None, DP, TENSOR)),
        check_vma=False,
    )
```

```python
import functools
import math

import jax
import jax.numpy as jnp
import numpy as np
from jax import lax
from jax.experimental import pallas as pl
from jax.experimental.pallas import tpu as pltpu
from jax.sharding import Mesh, PartitionSpec as P

NZ, NX, NY, NC = 8, 4, 8, 2
HD = 128
EPS = 1e-05
ROPE_BASE = 500000.0
DP = ("z", "x")
TENSOR = ("y", "c")
F32 = jnp.float32
BF16 = jnp.bfloat16
LOW = -1e30
VMEM_LIMIT = 63 * 2**20
MESH = pl.DeviceIdType.MESH


def dot(a, b):
    return jnp.dot(a, b, preferred_element_type=F32)


def angles(context):
    freq = np.power(np.float32(ROPE_BASE), -2.0 * np.arange(HD // 2, dtype=np.float32) / HD)
    freq = freq.astype(np.float32)
    step = (np.arange(16) // 4) % 2
    angle = (np.float32(context) + step.astype(np.float32))[:, None] * freq[None, :]
    cos, sin = np.cos(angle), np.sin(angle)
    both = np.stack([np.concatenate([cos, cos], 1), np.concatenate([-sin, sin], 1)])
    return jnp.asarray(both.astype(np.float32))


def iota(shape, dim):
    return lax.broadcasted_iota(jnp.int32, shape, dim)


def kernel(
    anc, x_first, x_second, attn_gain, ffn_gain, rope, ck, cv, wq, wkv, wo, wg, wu, wd,
    attn_out, ffn_out,
    xrow, select, select_t, local_row, wq_v, wkv_v, wo_v, wgu_v, wd_v,
    ga, gg, part, bcs, bcr, bys, byr, cs, cr, cache1, cache2,
    ds_, dr, rs, rr, es, er, mb, fxs, fxr, fzs, fzr, ixs, ixr, izs, izr,
    hown, hcs, hcr, hys, hyr, hid,
    lsem, kvsem, gaz, gax, ggz, ggx, bc, by, csem, c1, c2, dsem, rsem, esem, e2sem,
    fx, fz, ix, iz, hc, hy, h2y, h2c,
):
    z, x, y, c = (lax.axis_index(a) for a in ("z", "x", "y", "c"))
    width = x_first.shape[1] * NY * NC
    ff = wg.shape[0]
    finals = []

    def loop(low, high, body):
        def step(k, carry):
            body(k)
            return carry

        lax.fori_loop(low, high, step, 0)

    def remote(src, dst, sems, n, **where):
        return pltpu.make_async_remote_copy(
            src_ref=src, dst_ref=dst, send_sem=sems.at[0, 0], recv_sem=sems.at[1, n],
            device_id=where, device_id_type=MESH,
        )

    def arrived(ref, sems, n):
        pltpu.make_async_copy(ref, ref, sems.at[1, n]).wait()

    def sent(ref, sems):
        pltpu.make_async_copy(ref, ref, sems.at[0, 0]).wait()

    most = lambda ref, n: ref.at[pl.ds(0, n)]

    zk = lambda k: lax.rem(z + k, NZ)
    zb = lambda k: lax.rem(z + NZ - k, NZ)
    xk = lambda j: lax.rem(x + j, NX)
    xb = lambda j: lax.rem(x + NX - j, NX)
    yk = lambda k: lax.rem(y + k, NY)
    yb = lambda k: lax.rem(y + NY - k, NY)

    me = z * NX + x
    to_z, to_x = (me % 16) // 2, me // 16 * 2 + me % 2
    from_dp = x // 2 * 16 + 2 * z + x % 2
    from_z, from_x = from_dp // NX, from_dp % NX
    stays = from_dp == me
    barrier = pltpu.get_barrier_semaphore()

    def greet(**where):
        pl.semaphore_signal(barrier, inc=1, device_id=where, device_id_type=MESH)

    loop(1, 8, lambda k: greet(z=zk(k)))
    loop(1, 32, lambda n: greet(x=xk(n // 8), y=yk(n % 8)))
    loop(0, 4, lambda j: greet(x=xk(j), c=1 - c))
    loop(1, 8, lambda k: greet(y=yk(k), c=1 - c))

    @pl.when(jnp.logical_not(stays))
    def _():
        greet(z=to_z, x=to_x)
        greet(z=from_z, x=from_x)


    loads = [
        pltpu.make_async_copy(wq, wq_v, lsem.at[0]),
        pltpu.make_async_copy(wo, wo_v, lsem.at[1]),
        pltpu.make_async_copy(wg, wgu_v.at[pl.ds(0, ff)], lsem.at[2]),
        pltpu.make_async_copy(wu, wgu_v.at[pl.ds(512, ff)], lsem.at[3]),
        pltpu.make_async_copy(wd, wd_v.at[pl.ds(0, ff)], lsem.at[4]),
        pltpu.make_async_copy(ck.at[:, pl.ds(pl.multiple_of(z * HD, HD), HD)], cache1.at[z, 0], lsem.at[5]),
        pltpu.make_async_copy(cv.at[:, pl.ds(pl.multiple_of(z * HD, HD), HD)], cache1.at[z, 1], lsem.at[6]),
    ]
    for load in loads:
        load.start()
    r = iota((16, 16), 0)
    q = iota((16, 16), 1)
    order16 = jnp.where(q == (r // 4) % 2 * 8 + r // 8 * 4 + r % 4, 1.0, 0.0).astype(BF16)
    r_t, q_t = q, r
    back16 = jnp.where(q_t == (r_t // 4) % 2 * 8 + r_t // 8 * 4 + r_t % 4, 1.0, 0.0).astype(BF16)
    pair = jnp.concatenate([x_first[...].astype(F32), x_second[...].astype(F32)], axis=0)
    xrow[...] = dot(order16, pair.astype(BF16)).astype(BF16)
    ga[x, z] = xrow[...]

    pl.semaphore_wait(barrier, jnp.where(stays, 49, 51))

    def turn(i, first):
        return jnp.where(i == 0, 0, 1 + lax.rem(i + 6 + first, 7))

    def gather_begin(buf, zs, xs):
        block = buf.at[x, z]

        def one(i):
            k = turn(i, y)
            remote(block, block, zs, k, z=zk(k)).start()

        loop(1, 8, one)
        loop(1, 4, lambda j: remote(block, block, xs, 0, x=xk(j)).start())

    def dp_to_tensor(buf, zs, xs, work, own, csend, crecv, ysend, yrecv, cs_, ys_, also=None):
        def pass_on(i):
            k = turn(i, y)
            block = buf.at[x, zb(k)]
            arrived(block, zs, k)
            loop(1, 4, lambda j: remote(block, block, xs, k, x=xk(j)).start())

        def to_ring(i):
            n = zb(turn(i, y))
            arrived(crecv.at[n], cs_, n)

            @pl.when(n != y)
            def _():
                ysend[n] = (own(n) + crecv[n].astype(F32)).astype(BF16)
                remote(ysend.at[n], yrecv.at[y], ys_, 0, y=n).start()

        def body(i):
            k = turn(i, y)
            n = zb(k)
            pl.when(i < 6)(lambda: pass_on(i + 2))
            arrived(buf.at[pl.ds(0, 3), 0], xs, k)
            work(n)
            remote(csend.at[n], crecv.at[n], cs_, n, c=1 - c).start()
            pl.when(i >= 4)(lambda: to_ring(i - 4))
            if also is not None:
                pl.when(i == 4)(also)

        pass_on(1)
        loop(0, 8, body)
        loop(4, 8, to_ring)

        def close():
            sent(buf.at[0, pl.ds(0, 7)], zs)
            sent(most(buf, 3), xs)
            sent(csend, cs_)
            sent(most(ysend, 7), ys_)

        finals.append(close)

        def finish():
            acc = own(y) + crecv[y].astype(F32)
            arrived(most(yrecv, 7), ys_, 0)
            for k in range(1, 8):
                acc = acc + yrecv[yb(k)].astype(F32)
            return acc

        return finish

    def tensor_to_dp(ahead, work, xsend, xrecv, zsend, zrecv, xs, zs):
        def total(n):
            arrived(xrecv.at[pl.ds(0, 3), 0], xs, n)
            block = xsend[x, n].astype(F32)
            for j in range(1, 4):
                block = block + xrecv[xb(j), n].astype(F32)
            return block

        def to_ring(i):
            n = yb(turn(i, z))
            zsend[n] = total(n).astype(BF16)

            @pl.when(n != z)
            def _():
                remote(zsend.at[n], zrecv.at[z], zs, 0, z=n).start()

        def body(i):
            k = turn(i, z)
            n = yb(k)
            ahead(i, k, n)
            xsend[:, n] = work(n).astype(BF16).reshape(4, 16, 512)
            loop(1, 4, lambda j: remote(xsend.at[xk(j), n], xrecv.at[x, n], xs, n, x=xk(j)).start())
            pl.when(i >= 4)(lambda: to_ring(i - 4))

        loop(0, 8, body)
        loop(4, 8, to_ring)
        acc = zsend[z].astype(F32)
        arrived(most(zrecv, 7), zs, 0)
        for k in range(1, 8):
            acc = acc + zrecv[zb(k)].astype(F32)

        def close():
            sent(most(xsend, 3), xs)
            sent(most(zsend, 7), zs)

        finals.append(close)
        return acc

    gather_begin(ga, gaz, gax)

    @pl.when(stays)
    def _():
        pltpu.make_async_copy(wkv, wkv_v.at[pl.ds(0, 64)], kvsem.at[1, 0]).start()

    @pl.when(jnp.logical_not(stays))
    def _():
        remote(wkv, wkv_v.at[pl.ds(0, 64)], kvsem, 0, z=to_z, x=to_x).start()

    def cache_out(k):
        cols = pl.ds(pl.multiple_of(zk(k) * HD, HD), HD)
        remote(ck.at[:, cols], cache1.at[z, 0], c1, 0, z=zk(k)).start()
        remote(cv.at[:, cols], cache1.at[z, 1], c1, 0, z=zk(k)).start()

    loop(1, 8, cache_out)

    wd_v[pl.ds(ff, 512 - ff), :] = jnp.zeros((512 - ff, 512), BF16)
    wgu_v[pl.ds(ff, 512 - ff), :] = jnp.zeros((512 - ff, 512), BF16)
    wgu_v[pl.ds(512 + ff, 512 - ff), :] = jnp.zeros((512 - ff, 512), BF16)
    wkv_v[pl.ds(64, 64), :] = jnp.zeros((64, 512), BF16)
    mine = [anc[(y * NX + x) * 8 + p] for p in range(8)]
    codes = []
    for p in range(8):
        block = lax.shift_right_logical(mine[p], 3)
        place = (block & 3) * 8 + lax.shift_right_logical(block, 2)
        quad = lax.shift_right_logical(mine[p], 2)
        rank = jnp.int32(0)
        for other in range(p):
            rank = rank + jnp.where(lax.shift_right_logical(mine[other], 2) == quad, 1, 0)
        codes.append(place * 4 + (quad & 1) * 2 + rank)

    def per_particle(index, values):
        out = jnp.zeros(index.shape, jnp.int32)
        for p in range(8):
            out = jnp.where((index // 8) % 2 * 4 + index % 4 == p, values[p], out)
        return out

    def hits(row, col, code):
        hit = (col // 16 == row % 8) & ((col // 4) % 2 == 1)
        return jnp.where(hit & (code == row // 16 * 4 + c * 2 + row // 8 % 2), 1.0, 0.0).astype(BF16)

    select[...] = hits(iota((512, 128), 0), iota((512, 128), 1), per_particle(iota((1, 128), 1), codes))
    select_t[...] = hits(iota((128, 512), 1), iota((128, 512), 0), per_particle(iota((128, 1), 0), codes))
    spots = per_particle(iota((16, 128), 0), [m & 3 for m in mine])
    local_row[...] = spots.astype(F32).astype(BF16)
    loads[0].wait()
    arrived(wkv_v.at[pl.ds(0, 64)], kvsem, 0)

    lane = iota((64, 128), 1)

    def dot_t(a, b):
        return lax.dot_general(a, b, (((1,), (1,)), ((), ())), preferred_element_type=F32)

    def squares_of(wide):
        square = jnp.sum(wide * wide, axis=1, keepdims=True)
        hi = square.astype(BF16).astype(F32)
        return jnp.where(lane == 64, hi, 0.0) + jnp.where(lane == 65, square - hi, 0.0)

    def project(n):
        wide = ga[:, n].reshape(64, 512).astype(F32)
        scaled = (wide * attn_gain[...]).astype(BF16)
        part[n, :, :, :, 0:256] = dot(scaled, wq_v[...]).reshape(4, 2, 8, 256)
        part[n, :, :, :, 256:384] = (dot_t(scaled, wkv_v[...]) + squares_of(wide)).reshape(4, 2, 8, 128)
        bcs[n] = part[n, :, 1 - c].reshape(32, 384).astype(BF16)

    def cache_pass():
        loads[5].wait()
        loads[6].wait()

        arrived(most(cache1, 7), c1, 0)
        other = 1 - c
        keep = pltpu.make_async_copy(
            cache1.at[y, :, pl.ds(pl.multiple_of(c * 32, 32), 32), :], cache2.at[y * 2 + c], lsem.at[7]
        )
        keep.start()

        def pass_same(k):
            remote(
                cache1.at[yk(k), :, pl.ds(pl.multiple_of(c * 32, 32), 32), :], cache2.at[y * 2 + c],
                c2, 0, y=yk(k),
            ).start()

        loop(1, 8, pass_same)

        def pass_other(k):
            remote(
                cache1.at[yk(k), :, pl.ds(pl.multiple_of(other * 32, 32), 32), :], cache2.at[y * 2 + c],
                c2, 0, y=yk(k), c=other,
            ).start()

        loop(0, 8, pass_other)
        keep.wait()

    def close_cache():
        sent(most(cache1, 7), c1)
        sent(most(cache2, 15), c2)

        @pl.when(jnp.logical_not(stays))
        def _():
            sent(wkv_v.at[pl.ds(0, 64)], kvsem)

    finals.append(close_cache)

    finish = dp_to_tensor(
        ga, gaz, gax, project, lambda n: part[n, :, c].reshape(32, 384), bcs, bcr, bys, byr, bc, by, cache_pass
    )

    acc = finish()
    factor = lax.rsqrt((acc[:, 320:321] + acc[:, 321:322]) / width + EPS)
    cs[...] = (acc * factor).astype(BF16).astype(F32).reshape(4, 8, 384)

    def share(src, dst, sems):
        def one(n):
            j, to_c = n // 2, lax.rem(c + n % 2, 2)
            remote(src.at[xk(j)], dst.at[x * 2 + c], sems, 0, x=xk(j), c=to_c).start()

        dst[x * 2 + c] = src[x]
        loop(1, 8, one)
        arrived(most(dst, 7), sems, 0)
        finals.append(lambda: sent(most(dst, 7), sems))

    share(cs, cr, csem)

    def rotated(rows):
        count = rows.shape[0] // 16
        cos = jnp.concatenate([rope[0]] * count, axis=0)
        sin = jnp.concatenate([rope[1]] * count, axis=0)
        return (rows * cos + pltpu.roll(rows, 64, 1) * sin).astype(BF16)

    heads = [cr[2 * n : 2 * n + 2].reshape(16, 384) for n in range(4)]
    queries = rotated(
        jnp.concatenate([h[:, a : a + HD] for h in heads for a in (0, HD)], axis=0)
    )
    low = iota((16, HD), 1) < 64
    join = lambda a, b: jnp.where(low, a[:, 256:384], pltpu.roll(b[:, 256:384], 64, 1))
    new_keys = rotated(join(heads[0], heads[1]))
    new_values = join(heads[2], heads[3]).astype(BF16)

    spot = x * 8 + y
    pairs = jnp.concatenate(
        [new_keys, new_values, local_row[...], jnp.zeros((80, HD), BF16)], axis=0
    )
    ds_[:, :, 0:HD] = dot(select[...], queries).astype(BF16).reshape(32, 16, HD)
    ds_[:, :, HD : 2 * HD] = dot(select[...], pairs).astype(BF16).reshape(32, 16, HD)
    dr[spot] = ds_[spot]

    def trade(src, dst, sems):
        def one(n):
            px, py = xk(n // 8), yk(n % 8)
            remote(src.at[px * 8 + py], dst.at[spot], sems, 0, x=px, y=py).start()

        loop(1, 32, one)
        finals.append(lambda: sent(most(src, 31), sems))

    def traded(dst, sems):
        arrived(most(dst, 31), sems, 0)

    trade(ds_, dr, dsem)
    arrived(most(cache2, 15), c2, 0)
    traded(dr, dsem)

    tail = dr[:, :, HD : 2 * HD].astype(F32).reshape(64, 8, HD)
    every_head = lambda n: jnp.broadcast_to(tail[:, n : n + 1, :], (64, 8, HD)).reshape(512, HD)
    own_key, own_value = every_head(0), every_head(1)
    which = jnp.concatenate([every_head(2)[:, 0:1], (iota((128, 1), 0) % 4).astype(F32)], axis=0)
    asked = jnp.concatenate([dr[:, :, 0:HD].reshape(512, HD), queries], axis=0)
    pad = jnp.zeros((112, HD), BF16)
    keys = jnp.concatenate([cache2[:, 0].reshape(512, HD), new_keys, pad], axis=0)
    values = jnp.concatenate([cache2[:, 1].reshape(512, HD), new_values, pad], axis=0)
    scale = 1.0 / math.sqrt(HD)
    scores = lax.dot_general(asked, keys, (((1,), (1,)), ((), ())), preferred_element_type=F32)
    k = iota((1, 640), 1)
    new = k - 512
    key_particle = jnp.where(k < 512, (k // 8) % 4, k % 4)
    key_ok = (k < 512) | ((new < 16) & ((new // 4) % 2 == 0) & (new // 8 == c))
    key_particle = jnp.where(key_ok, key_particle, -1).astype(F32)
    scores = jnp.where(key_particle == which, scores * scale, LOW)
    own = jnp.sum(asked[0:512].astype(F32) * own_key, axis=1, keepdims=True) * scale
    own = jnp.concatenate([own, jnp.full((128, 1), LOW, F32)], axis=0)
    highest = jnp.maximum(jnp.max(scores, axis=1, keepdims=True), own)
    weights = jnp.exp(scores - highest)
    own = jnp.exp(own - highest)
    totals = jnp.sum(weights, axis=1, keepdims=True) + own
    mixed = dot(weights.astype(BF16), values)
    extra = jnp.concatenate([own[0:512] * own_value, jnp.zeros((128, HD), F32)], axis=0)
    mixed = (mixed + extra) / totals

    rs[...] = mixed[0:512].astype(BF16).reshape(32, 16, HD)
    rr[spot] = rs[spot]
    trade(rs, rr, rsem)
    r = iota((128, 1), 0)
    first = jnp.where(((r // 4) % 2 == 0) & ((r // 8) % 2 == c), mixed[512:640], 0.0)
    traded(rr, rsem)
    both = (first + dot(select_t[...], rr[...].reshape(512, HD))).astype(BF16)
    for n in range(4):
        es[n, :, 0:HD] = both[n * 32 : n * 32 + 16]
        es[n, :, HD : 2 * HD] = both[n * 32 + 16 : n * 32 + 32]
    share(es, er, esem)
    for n in range(4):
        mb[y, n * 16 : n * 16 + 16, :] = (er[2 * n].astype(F32) + er[2 * n + 1].astype(F32)).astype(BF16)


    def rows_out(i):
        k = turn(i, z)
        remote(mb.at[y], mb.at[y], e2sem, k, y=yk(k)).start()

    loop(1, 8, rows_out)
    finals.append(lambda: sent(most(mb, 7), e2sem))
    loads[1].wait()

    def rows_came(i, k, n):
        pl.when(i > 0)(lambda: arrived(mb.at[n], e2sem, k))

    attn = tensor_to_dp(
        rows_came, lambda n: dot(mb[n], wo_v[...]), fxs, fxr, fzs, fzr, fx, fz
    ).astype(BF16)
    gg[x, z] = (xrow[...].astype(F32) + attn.astype(F32)).astype(BF16)

    gather_begin(gg, ggz, ggx)

    def give(out, block):
        turned = dot(back16, block)
        out[0] = turned[0:8].astype(BF16)
        out[1] = turned[8:16].astype(BF16)

    give(attn_out, attn)
    loads[2].wait()
    loads[3].wait()

    def gate_up(n):
        away = gg[pl.ds(2 * (1 - c), 2), n].reshape(32, 512)
        here = gg[pl.ds(2 * c, 2), n].reshape(32, 512)
        wide = jnp.concatenate([away, here], axis=0).astype(F32)
        scaled = (wide * ffn_gain[...]).astype(BF16)
        value = dot_t(scaled, wgu_v[...])
        mid = value[:, 384:512] + squares_of(wide)
        hcs[n] = value[0:32].astype(BF16)
        hcs[n, :, 384:512] = mid[0:32].astype(BF16)
        hown[n] = value[32:64]
        hown[n, :, 384:512] = mid[32:64]

    acc = dp_to_tensor(
        gg, ggz, ggx, gate_up, lambda n: hown[n], hcs, hcr, hys, hyr, hc, hy
    )()
    factor = lax.rsqrt((acc[:, ff : ff + 1] + acc[:, ff + 1 : ff + 2]) / width + EPS)
    gate, up = acc[:, 0:512] * factor, acc[:, 512:1024] * factor
    hidden = gate / (1.0 + jnp.exp(-gate)) * up
    hid[c, y] = jnp.where(iota((32, 512), 1) < ff, hidden, 0.0).astype(BF16)

    remote(hid.at[c, y], hid.at[c, y], h2c, 0, c=1 - c).start()

    def hidden_out(i):
        k = turn(i, z)
        remote(hid.at[c, y], hid.at[c, y], h2y, k, y=yk(k)).start()

    loop(1, 8, hidden_out)
    loads[4].wait()

    def pass_hidden(i):
        k = turn(i, z)
        block = hid.at[c, yb(k)]
        arrived(block, h2y, k)
        remote(block, block, h2c, k, c=1 - c).start()

    def hidden_came(i, k, n):
        pl.when(i < 7)(lambda: pass_hidden(i + 1))
        arrived(hid.at[1 - c, n], h2c, k)

    ffn = tensor_to_dp(
        hidden_came, lambda n: dot(hid[:, n].reshape(64, 512), wd_v[...]), ixs, ixr, izs, izr, ix, iz
    )
    give(ffn_out, ffn.astype(BF16))

    sent(hid.at[0, pl.ds(0, 7)], h2y)
    sent(hid.at[0], h2c)
    for close in finals:
        close()


def local(
    x_first, x_second, cache_keys, cache_values, ancestors, attn_gain, ffn_gain,
    w_query, w_keyval, w_out, w_gate, w_up, w_down,
):
    context = cache_keys.shape[1] * NY * NC
    v = lambda *shape: pltpu.VMEM(shape, BF16)
    f = lambda *shape: pltpu.VMEM(shape, F32)
    sem = lambda n: pltpu.SemaphoreType.DMA((2, n))
    near, far = pl.BlockSpec(memory_space=pltpu.VMEM), pl.BlockSpec(memory_space=pl.ANY)
    big = [v(4, 8, 16, 512), v(4, 8, 16, 512), v(8, 16, 512), v(8, 16, 512)]
    return pl.pallas_call(
        kernel,
        out_shape=[jax.ShapeDtypeStruct((2, 8, 512), BF16)] * 2,
        in_specs=[pl.BlockSpec(memory_space=pltpu.SMEM)] + [near] * 5 + [far] * 8,
        out_specs=[near, near],
        scratch_shapes=[
            v(16, 512), v(512, 128), v(128, 512), v(16, HD),
            v(512, 256), v(128, 512), v(256, 512), v(1024, 512), v(512, 512),
            v(4, 8, 16, 512), v(4, 8, 16, 512), f(8, 4, 2, 8, 384),
            *[v(8, 32, 384)] * 4,
            f(4, 8, 384), f(8, 8, 384), v(8, 2, 64, HD), v(16, 2, 32, HD),
            v(32, 16, 256), v(32, 16, 256), v(32, 16, HD), v(32, 16, HD),
            v(4, 16, 256), v(8, 16, 256), v(8, 64, 256),
            *big, *big,
            f(8, 32, 1024), *[v(8, 32, 1024)] * 4, v(2, 8, 32, 512),
            pltpu.SemaphoreType.DMA((8,)), sem(1), sem(8), sem(32), sem(8), sem(32), sem(8), sem(8),
            sem(8), sem(16), sem(16), sem(32), sem(32), sem(8), sem(8),
            sem(32), sem(8), sem(32), sem(8), sem(8), sem(8), sem(8), sem(8),
        ],
        compiler_params=pltpu.CompilerParams(
            collective_id=0, has_side_effects=True, vmem_limit_bytes=VMEM_LIMIT
        ),
        cost_estimate=pl.CostEstimate(flops=2**30, bytes_accessed=2**22, transcendentals=2**19),
    )(
        ancestors, x_first, x_second, attn_gain[None], ffn_gain[None], angles(context),
        cache_keys.reshape(64, -1), cache_values.reshape(64, -1),
        w_query, w_keyval.T, w_out, w_gate.T, w_up.T, w_down,
    )


def solution(mesh):
    fine = Mesh(mesh.devices.reshape(NZ, NX, NY, NC), ("z", "x", "y", "c"))
    rows, cols = P(TENSOR, DP), P(DP, TENSOR)
    return jax.shard_map(
        local,
        mesh=fine,
        in_specs=(
            cols, cols, P(DP, TENSOR, None), P(DP, TENSOR, None), P(), P(TENSOR), P(TENSOR),
            rows, rows, cols, rows, rows, cols,
        ),
        out_specs=(P(None, DP, TENSOR), P(None, DP, TENSOR)),
        check_vma=False,
    )
```

```python
import functools
import math

import jax
import jax.numpy as jnp
import numpy as np
from jax import lax
from jax.experimental import pallas as pl
from jax.experimental.pallas import tpu as pltpu
from jax.sharding import Mesh, PartitionSpec as P

NZ, NX, NY, NC = 8, 4, 8, 2
HD = 128
EPS = 1e-05
ROPE_BASE = 500000.0
DP = ("z", "x")
TENSOR = ("y", "c")
F32 = jnp.float32
BF16 = jnp.bfloat16
LOW = -1e30
VMEM_LIMIT = 63 * 2**20
MESH = pl.DeviceIdType.MESH


def dot(a, b):
    return jnp.dot(a, b, preferred_element_type=F32)


def angles(context):
    freq = np.power(np.float32(ROPE_BASE), -2.0 * np.arange(HD // 2, dtype=np.float32) / HD)
    freq = freq.astype(np.float32)
    step = (np.arange(16) // 4) % 2
    angle = (np.float32(context) + step.astype(np.float32))[:, None] * freq[None, :]
    cos, sin = np.cos(angle), np.sin(angle)
    both = np.stack([np.concatenate([cos, cos], 1), np.concatenate([-sin, sin], 1)])
    return jnp.asarray(both.astype(np.float32))


def iota(shape, dim):
    return lax.broadcasted_iota(jnp.int32, shape, dim)


def kernel(
    anc, x_first, x_second, attn_gain, ffn_gain, rope, ck, cv, wq, wkv, wo, wg, wu, wd,
    attn_out, ffn_out,
    xrow, select, select_t, local_row, wq_v, wkv_v, wo_v, wgu_v, wd_v,
    ga, gg, part, bcs, bcr, bys, byr, cs, cr, cache1, cache2,
    ds_, dr, rs, rr, es, er, mb, fxs, fxr, fzs, fzr, ixs, ixr, izs, izr,
    hown, hcs, hcr, hys, hyr, hid,
    lsem, kvsem, gaz, gax, ggz, ggx, bc, by, csem, c1, c2, dsem, rsem, esem, e2sem,
    fx, fz, ix, iz, hc, hy, h2y, h2c, e2c,
):
    z, x, y, c = (lax.axis_index(a) for a in ("z", "x", "y", "c"))
    width = x_first.shape[1] * NY * NC
    ff = wg.shape[0]
    finals = []

    def loop(low, high, body):
        def step(k, carry):
            body(k)
            return carry

        lax.fori_loop(low, high, step, 0)

    def remote(src, dst, sems, n, **where):
        return pltpu.make_async_remote_copy(
            src_ref=src, dst_ref=dst, send_sem=sems.at[0, 0], recv_sem=sems.at[1, n],
            device_id=where, device_id_type=MESH,
        )

    def arrived(ref, sems, n):
        pltpu.make_async_copy(ref, ref, sems.at[1, n]).wait()

    def sent(ref, sems):
        pltpu.make_async_copy(ref, ref, sems.at[0, 0]).wait()

    most = lambda ref, n: ref.at[pl.ds(0, n)]

    zk = lambda k: lax.rem(z + k, NZ)
    zb = lambda k: lax.rem(z + NZ - k, NZ)
    xk = lambda j: lax.rem(x + j, NX)
    xb = lambda j: lax.rem(x + NX - j, NX)
    yk = lambda k: lax.rem(y + k, NY)
    yb = lambda k: lax.rem(y + NY - k, NY)

    me = z * NX + x
    to_z, to_x = (me % 16) // 2, me // 16 * 2 + me % 2
    from_dp = x // 2 * 16 + 2 * z + x % 2
    from_z, from_x = from_dp // NX, from_dp % NX
    stays = from_dp == me
    barrier = pltpu.get_barrier_semaphore()

    def greet(**where):
        pl.semaphore_signal(barrier, inc=1, device_id=where, device_id_type=MESH)

    loop(1, 8, lambda k: greet(z=zk(k)))
    loop(1, 32, lambda n: greet(x=xk(n // 8), y=yk(n % 8)))
    loop(0, 4, lambda j: greet(x=xk(j), c=1 - c))
    loop(1, 8, lambda k: greet(y=yk(k), c=1 - c))

    @pl.when(jnp.logical_not(stays))
    def _():
        greet(z=to_z, x=to_x)
        greet(z=from_z, x=from_x)


    loads = [
        pltpu.make_async_copy(wq, wq_v, lsem.at[0]),
        pltpu.make_async_copy(wo, wo_v, lsem.at[1]),
        pltpu.make_async_copy(wg, wgu_v.at[pl.ds(0, ff)], lsem.at[2]),
        pltpu.make_async_copy(wu, wgu_v.at[pl.ds(512, ff)], lsem.at[3]),
        pltpu.make_async_copy(wd, wd_v.at[pl.ds(0, ff)], lsem.at[4]),
        pltpu.make_async_copy(ck.at[:, pl.ds(pl.multiple_of(z * HD, HD), HD)], cache1.at[z, 0], lsem.at[5]),
        pltpu.make_async_copy(cv.at[:, pl.ds(pl.multiple_of(z * HD, HD), HD)], cache1.at[z, 1], lsem.at[6]),
    ]
    for load in loads:
        load.start()
    r = iota((16, 16), 0)
    q = iota((16, 16), 1)
    order16 = jnp.where(q == (r // 4) % 2 * 8 + r // 8 * 4 + r % 4, 1.0, 0.0).astype(BF16)
    r_t, q_t = q, r
    back16 = jnp.where(q_t == (r_t // 4) % 2 * 8 + r_t // 8 * 4 + r_t % 4, 1.0, 0.0).astype(BF16)
    pair = jnp.concatenate([x_first[...].astype(F32), x_second[...].astype(F32)], axis=0)
    xrow[...] = dot(order16, pair.astype(BF16)).astype(BF16)
    ga[x, z] = xrow[...]

    pl.semaphore_wait(barrier, jnp.where(stays, 49, 51))

    def turn(i, first):
        return jnp.where(i == 0, 0, 1 + lax.rem(i + 6 + first, 7))

    def gather_begin(buf, zs, xs):
        block = buf.at[x, z]

        def one(i):
            k = turn(i, y)
            remote(block, block, zs, k, z=zk(k)).start()

        loop(1, 8, one)
        loop(1, 4, lambda j: remote(block, block, xs, 0, x=xk(j)).start())

    def dp_to_tensor(buf, zs, xs, work, own, csend, crecv, ysend, yrecv, cs_, ys_, also=None):
        def pass_on(i):
            k = turn(i, y)
            block = buf.at[x, zb(k)]
            arrived(block, zs, k)
            loop(1, 4, lambda j: remote(block, block, xs, k, x=xk(j)).start())

        def to_ring(i):
            n = zb(turn(i, y))
            arrived(crecv.at[n], cs_, n)

            @pl.when(n != y)
            def _():
                ysend[n] = (own(n) + crecv[n].astype(F32)).astype(BF16)
                remote(ysend.at[n], yrecv.at[y], ys_, 0, y=n).start()

        def body(i):
            k = turn(i, y)
            n = zb(k)
            pl.when(i < 6)(lambda: pass_on(i + 2))
            arrived(buf.at[pl.ds(0, 3), 0], xs, k)
            work(n)
            remote(csend.at[n], crecv.at[n], cs_, n, c=1 - c).start()
            pl.when(i >= 4)(lambda: to_ring(i - 4))
            if also is not None:
                pl.when(i == 2)(also)

        pass_on(1)
        loop(0, 8, body)
        loop(4, 8, to_ring)

        def close():
            sent(buf.at[0, pl.ds(0, 7)], zs)
            sent(most(buf, 3), xs)
            sent(csend, cs_)
            sent(most(ysend, 7), ys_)

        finals.append(close)

        def finish():
            acc = own(y) + crecv[y].astype(F32)
            arrived(most(yrecv, 7), ys_, 0)
            for k in range(1, 8):
                acc = acc + yrecv[yb(k)].astype(F32)
            return acc

        return finish

    def tensor_to_dp(ahead, work, xsend, xrecv, zsend, zrecv, xs, zs):
        def total(n):
            arrived(xrecv.at[pl.ds(0, 3), 0], xs, n)
            block = xsend[x, n].astype(F32)
            for j in range(1, 4):
                block = block + xrecv[xb(j), n].astype(F32)
            return block

        def to_ring(i):
            n = yb(turn(i, z))
            zsend[n] = total(n).astype(BF16)

            @pl.when(n != z)
            def _():
                remote(zsend.at[n], zrecv.at[z], zs, 0, z=n).start()

        def body(i):
            k = turn(i, z)
            n = yb(k)
            ahead(i, k, n)
            xsend[:, n] = work(n).astype(BF16).reshape(4, 16, 512)
            loop(1, 4, lambda j: remote(xsend.at[xk(j), n], xrecv.at[x, n], xs, n, x=xk(j)).start())
            pl.when(i >= 4)(lambda: to_ring(i - 4))

        loop(0, 8, body)
        loop(4, 8, to_ring)
        acc = zsend[z].astype(F32)
        arrived(most(zrecv, 7), zs, 0)
        for k in range(1, 8):
            acc = acc + zrecv[zb(k)].astype(F32)

        def close():
            sent(most(xsend, 3), xs)
            sent(most(zsend, 7), zs)

        finals.append(close)
        return acc

    gather_begin(ga, gaz, gax)

    @pl.when(stays)
    def _():
        pltpu.make_async_copy(wkv, wkv_v.at[pl.ds(0, 64)], kvsem.at[1, 0]).start()

    @pl.when(jnp.logical_not(stays))
    def _():
        remote(wkv, wkv_v.at[pl.ds(0, 64)], kvsem, 0, z=to_z, x=to_x).start()

    def cache_out(k):
        cols = pl.ds(pl.multiple_of(zk(k) * HD, HD), HD)
        remote(ck.at[:, cols], cache1.at[z, 0], c1, 0, z=zk(k)).start()
        remote(cv.at[:, cols], cache1.at[z, 1], c1, 0, z=zk(k)).start()

    loop(1, 8, cache_out)

    wd_v[pl.ds(ff, 512 - ff), :] = jnp.zeros((512 - ff, 512), BF16)
    wgu_v[pl.ds(ff, 512 - ff), :] = jnp.zeros((512 - ff, 512), BF16)
    wgu_v[pl.ds(512 + ff, 512 - ff), :] = jnp.zeros((512 - ff, 512), BF16)
    wkv_v[pl.ds(64, 64), :] = jnp.zeros((64, 512), BF16)
    mine = [anc[(y * NX + x) * 8 + p] for p in range(8)]
    codes = []
    for p in range(8):
        block = lax.shift_right_logical(mine[p], 3)
        place = (block & 3) * 8 + lax.shift_right_logical(block, 2)
        quad = lax.shift_right_logical(mine[p], 2)
        rank = jnp.int32(0)
        for other in range(p):
            rank = rank + jnp.where(lax.shift_right_logical(mine[other], 2) == quad, 1, 0)
        codes.append(place * 4 + (quad & 1) * 2 + rank)

    def per_particle(index, values):
        out = jnp.zeros(index.shape, jnp.int32)
        for p in range(8):
            out = jnp.where((index // 8) % 2 * 4 + index % 4 == p, values[p], out)
        return out

    def hits(row, col, code):
        hit = (col // 16 == row % 8) & ((col // 4) % 2 == 1)
        return jnp.where(hit & (code == row // 16 * 4 + c * 2 + row // 8 % 2), 1.0, 0.0).astype(BF16)

    select[...] = hits(iota((512, 128), 0), iota((512, 128), 1), per_particle(iota((1, 128), 1), codes))
    select_t[...] = hits(iota((128, 512), 1), iota((128, 512), 0), per_particle(iota((128, 1), 0), codes))
    spots = per_particle(iota((16, 128), 0), [m & 3 for m in mine])
    local_row[...] = spots.astype(F32).astype(BF16)
    loads[0].wait()
    arrived(wkv_v.at[pl.ds(0, 64)], kvsem, 0)

    lane = iota((64, 128), 1)

    def dot_t(a, b):
        return lax.dot_general(a, b, (((1,), (1,)), ((), ())), preferred_element_type=F32)

    def squares_of(wide):
        square = jnp.sum(wide * wide, axis=1, keepdims=True)
        hi = square.astype(BF16).astype(F32)
        return jnp.where(lane == 64, hi, 0.0) + jnp.where(lane == 65, square - hi, 0.0)

    def project(n):
        wide = ga[:, n].reshape(64, 512).astype(F32)
        scaled = (wide * attn_gain[...]).astype(BF16)
        part[n, :, :, :, 0:256] = dot(scaled, wq_v[...]).reshape(4, 2, 8, 256)
        part[n, :, :, :, 256:384] = (dot_t(scaled, wkv_v[...]) + squares_of(wide)).reshape(4, 2, 8, 128)
        bcs[n] = part[n, :, 1 - c].reshape(32, 384).astype(BF16)

    def cache_pass():
        loads[5].wait()
        loads[6].wait()

        arrived(most(cache1, 7), c1, 0)
        other = 1 - c
        keep = pltpu.make_async_copy(
            cache1.at[y, :, pl.ds(pl.multiple_of(c * 32, 32), 32), :], cache2.at[y * 2 + c], lsem.at[7]
        )
        keep.start()

        def pass_same(k):
            remote(
                cache1.at[yk(k), :, pl.ds(pl.multiple_of(c * 32, 32), 32), :], cache2.at[y * 2 + c],
                c2, 0, y=yk(k),
            ).start()

        loop(1, 8, pass_same)

        def pass_other(k):
            remote(
                cache1.at[yk(k), :, pl.ds(pl.multiple_of(other * 32, 32), 32), :], cache2.at[y * 2 + c],
                c2, 0, y=yk(k), c=other,
            ).start()

        loop(0, 8, pass_other)
        keep.wait()

    def close_cache():
        sent(most(cache1, 7), c1)
        sent(most(cache2, 15), c2)

        @pl.when(jnp.logical_not(stays))
        def _():
            sent(wkv_v.at[pl.ds(0, 64)], kvsem)

    finals.append(close_cache)

    finish = dp_to_tensor(
        ga, gaz, gax, project, lambda n: part[n, :, c].reshape(32, 384), bcs, bcr, bys, byr, bc, by, cache_pass
    )

    acc = finish()
    factor = lax.rsqrt((acc[:, 320:321] + acc[:, 321:322]) / width + EPS)
    cs[...] = (acc * factor).astype(BF16).astype(F32).reshape(4, 8, 384)

    def share(src, dst, sems):
        def one(n):
            j, to_c = n // 2, lax.rem(c + n % 2, 2)
            remote(src.at[xk(j)], dst.at[x * 2 + c], sems, 0, x=xk(j), c=to_c).start()

        dst[x * 2 + c] = src[x]
        loop(1, 8, one)
        arrived(most(dst, 7), sems, 0)
        finals.append(lambda: sent(most(dst, 7), sems))

    share(cs, cr, csem)

    def rotated(rows):
        count = rows.shape[0] // 16
        cos = jnp.concatenate([rope[0]] * count, axis=0)
        sin = jnp.concatenate([rope[1]] * count, axis=0)
        return (rows * cos + pltpu.roll(rows, 64, 1) * sin).astype(BF16)

    heads = [cr[2 * n : 2 * n + 2].reshape(16, 384) for n in range(4)]
    queries = rotated(
        jnp.concatenate([h[:, a : a + HD] for h in heads for a in (0, HD)], axis=0)
    )
    low = iota((16, HD), 1) < 64
    join = lambda a, b: jnp.where(low, a[:, 256:384], pltpu.roll(b[:, 256:384], 64, 1))
    new_keys = rotated(join(heads[0], heads[1]))
    new_values = join(heads[2], heads[3]).astype(BF16)

    spot = x * 8 + y
    pairs = jnp.concatenate(
        [new_keys, new_values, local_row[...], jnp.zeros((80, HD), BF16)], axis=0
    )
    ds_[:, :, 0:HD] = dot(select[...], queries).astype(BF16).reshape(32, 16, HD)
    ds_[:, :, HD : 2 * HD] = dot(select[...], pairs).astype(BF16).reshape(32, 16, HD)
    dr[spot] = ds_[spot]

    def trade(src, dst, sems):
        def one(n):
            px, py = xk(n // 8), yk(n % 8)
            remote(src.at[px * 8 + py], dst.at[spot], sems, 0, x=px, y=py).start()

        loop(1, 32, one)
        finals.append(lambda: sent(most(src, 31), sems))

    def traded(dst, sems):
        arrived(most(dst, 31), sems, 0)

    trade(ds_, dr, dsem)
    arrived(most(cache2, 15), c2, 0)
    traded(dr, dsem)

    tail = dr[:, :, HD : 2 * HD].astype(F32).reshape(64, 8, HD)
    every_head = lambda n: jnp.broadcast_to(tail[:, n : n + 1, :], (64, 8, HD)).reshape(512, HD)
    own_key, own_value = every_head(0), every_head(1)
    which = jnp.concatenate([every_head(2)[:, 0:1], (iota((128, 1), 0) % 4).astype(F32)], axis=0)
    asked = jnp.concatenate([dr[:, :, 0:HD].reshape(512, HD), queries], axis=0)
    pad = jnp.zeros((112, HD), BF16)
    keys = jnp.concatenate([cache2[:, 0].reshape(512, HD), new_keys, pad], axis=0)
    values = jnp.concatenate([cache2[:, 1].reshape(512, HD), new_values, pad], axis=0)
    scale = 1.0 / math.sqrt(HD)
    scores = lax.dot_general(asked, keys, (((1,), (1,)), ((), ())), preferred_element_type=F32)
    k = iota((1, 640), 1)
    new = k - 512
    key_particle = jnp.where(k < 512, (k // 8) % 4, k % 4)
    key_ok = (k < 512) | ((new < 16) & ((new // 4) % 2 == 0) & (new // 8 == c))
    key_particle = jnp.where(key_ok, key_particle, -1).astype(F32)
    scores = jnp.where(key_particle == which, scores * scale, LOW)
    own = jnp.sum(asked[0:512].astype(F32) * own_key, axis=1, keepdims=True) * scale
    own = jnp.concatenate([own, jnp.full((128, 1), LOW, F32)], axis=0)
    highest = jnp.maximum(jnp.max(scores, axis=1, keepdims=True), own)
    weights = jnp.exp(scores - highest)
    own = jnp.exp(own - highest)
    totals = jnp.sum(weights, axis=1, keepdims=True) + own
    mixed = dot(weights.astype(BF16), values)
    extra = jnp.concatenate([own[0:512] * own_value, jnp.zeros((128, HD), F32)], axis=0)
    mixed = (mixed + extra) / totals

    rs[...] = mixed[0:512].astype(BF16).reshape(32, 16, HD)
    rr[spot] = rs[spot]
    trade(rs, rr, rsem)
    r = iota((128, 1), 0)
    first = jnp.where(((r // 4) % 2 == 0) & ((r // 8) % 2 == c), mixed[512:640], 0.0)
    traded(rr, rsem)
    both = (first + dot(select_t[...], rr[...].reshape(512, HD))).astype(BF16)
    for n in range(4):
        es[n, :, 0:HD] = both[n * 32 : n * 32 + 16]
        es[n, :, HD : 2 * HD] = both[n * 32 + 16 : n * 32 + 32]
    share(es, er, esem)
    for n in range(2):
        first, second = er[4 * c + 2 * n].astype(F32), er[4 * c + 2 * n + 1].astype(F32)
        mb[c, y, n * 16 : n * 16 + 16, :] = (first + second).astype(BF16)

    def tensor_begin(buf, ys_, cs_):
        block = buf.at[c, y]
        remote(block, block, cs_, 0, c=1 - c).start()

        def one(i):
            k = turn(i, z)
            remote(block, block, ys_, k, y=yk(k)).start()

        loop(1, 8, one)
        finals.append(lambda: sent(buf.at[0, pl.ds(0, 7)], ys_))
        finals.append(lambda: sent(buf.at[0], cs_))

    def tensor_came(buf, ys_, cs_):
        def pass_core(i):
            k = turn(i, z)
            block = buf.at[c, yb(k)]
            arrived(block, ys_, k)
            remote(block, block, cs_, k, c=1 - c).start()

        def came(i, k, n):
            pl.when(i < 7)(lambda: pass_core(i + 1))
            arrived(buf.at[1 - c, n], cs_, k)

        return came

    tensor_begin(mb, e2sem, e2c)
    loads[1].wait()

    attn = tensor_to_dp(
        tensor_came(mb, e2sem, e2c), lambda n: dot(mb[:, n].reshape(64, 256), wo_v[...]), fxs, fxr, fzs, fzr, fx, fz
    ).astype(BF16)
    gg[x, z] = (xrow[...].astype(F32) + attn.astype(F32)).astype(BF16)

    gather_begin(gg, ggz, ggx)

    def give(out, block):
        turned = dot(back16, block)
        out[0] = turned[0:8].astype(BF16)
        out[1] = turned[8:16].astype(BF16)

    give(attn_out, attn)
    loads[2].wait()
    loads[3].wait()

    def gate_up(n):
        away = gg[pl.ds(2 * (1 - c), 2), n].reshape(32, 512)
        here = gg[pl.ds(2 * c, 2), n].reshape(32, 512)
        wide = jnp.concatenate([away, here], axis=0).astype(F32)
        scaled = (wide * ffn_gain[...]).astype(BF16)
        value = dot_t(scaled, wgu_v[...])
        mid = value[:, 384:512] + squares_of(wide)
        hcs[n] = value[0:32].astype(BF16)
        hcs[n, :, 384:512] = mid[0:32].astype(BF16)
        hown[n] = value[32:64]
        hown[n, :, 384:512] = mid[32:64]

    acc = dp_to_tensor(
        gg, ggz, ggx, gate_up, lambda n: hown[n], hcs, hcr, hys, hyr, hc, hy
    )()
    factor = lax.rsqrt((acc[:, ff : ff + 1] + acc[:, ff + 1 : ff + 2]) / width + EPS)
    gate, up = acc[:, 0:512] * factor, acc[:, 512:1024] * factor
    hidden = gate / (1.0 + jnp.exp(-gate)) * up
    hid[c, y] = jnp.where(iota((32, 512), 1) < ff, hidden, 0.0).astype(BF16)

    tensor_begin(hid, h2y, h2c)
    loads[4].wait()

    ffn = tensor_to_dp(
        tensor_came(hid, h2y, h2c), lambda n: dot(hid[:, n].reshape(64, 512), wd_v[...]), ixs, ixr, izs, izr, ix, iz
    )
    give(ffn_out, ffn.astype(BF16))

    for close in finals:
        close()


def local(
    x_first, x_second, cache_keys, cache_values, ancestors, attn_gain, ffn_gain,
    w_query, w_keyval, w_out, w_gate, w_up, w_down,
):
    context = cache_keys.shape[1] * NY * NC
    v = lambda *shape: pltpu.VMEM(shape, BF16)
    f = lambda *shape: pltpu.VMEM(shape, F32)
    sem = lambda n: pltpu.SemaphoreType.DMA((2, n))
    near, far = pl.BlockSpec(memory_space=pltpu.VMEM), pl.BlockSpec(memory_space=pl.ANY)
    big = [v(4, 8, 16, 512), v(4, 8, 16, 512), v(8, 16, 512), v(8, 16, 512)]
    return pl.pallas_call(
        kernel,
        out_shape=[jax.ShapeDtypeStruct((2, 8, 512), BF16)] * 2,
        in_specs=[pl.BlockSpec(memory_space=pltpu.SMEM)] + [near] * 5 + [far] * 8,
        out_specs=[near, near],
        scratch_shapes=[
            v(16, 512), v(512, 128), v(128, 512), v(16, HD),
            v(512, 256), v(128, 512), v(256, 512), v(1024, 512), v(512, 512),
            v(4, 8, 16, 512), v(4, 8, 16, 512), f(8, 4, 2, 8, 384),
            *[v(8, 32, 384)] * 4,
            f(4, 8, 384), f(8, 8, 384), v(8, 2, 64, HD), v(16, 2, 32, HD),
            v(32, 16, 256), v(32, 16, 256), v(32, 16, HD), v(32, 16, HD),
            v(4, 16, 256), v(8, 16, 256), v(2, 8, 32, 256),
            *big, *big,
            f(8, 32, 1024), *[v(8, 32, 1024)] * 4, v(2, 8, 32, 512),
            pltpu.SemaphoreType.DMA((8,)), sem(1), sem(8), sem(32), sem(8), sem(32), sem(8), sem(8),
            sem(8), sem(16), sem(16), sem(32), sem(32), sem(8), sem(8),
            sem(32), sem(8), sem(32), sem(8), sem(8), sem(8), sem(8), sem(8), sem(8),
        ],
        compiler_params=pltpu.CompilerParams(
            collective_id=0, has_side_effects=True, vmem_limit_bytes=VMEM_LIMIT
        ),
        cost_estimate=pl.CostEstimate(flops=2**30, bytes_accessed=2**22, transcendentals=2**19),
    )(
        ancestors, x_first, x_second, attn_gain[None], ffn_gain[None], angles(context),
        cache_keys.reshape(64, -1), cache_values.reshape(64, -1),
        w_query, w_keyval.T, w_out, w_gate.T, w_up.T, w_down,
    )


def solution(mesh):
    fine = Mesh(mesh.devices.reshape(NZ, NX, NY, NC), ("z", "x", "y", "c"))
    rows, cols = P(TENSOR, DP), P(DP, TENSOR)
    return jax.shard_map(
        local,
        mesh=fine,
        in_specs=(
            cols, cols, P(DP, TENSOR, None), P(DP, TENSOR, None), P(), P(TENSOR), P(TENSOR),
            rows, rows, cols, rows, rows, cols,
        ),
        out_specs=(P(None, DP, TENSOR), P(None, DP, TENSOR)),
        check_vma=False,
    )
```
